256 devices in a mesh: dp: 4 (over x), frame: 32 (over z, y), spatial: 2 (over core).
Axes of the slice: x: 4, y: 4, z: 8, core: 2. Of those that a mesh axis runs over, the one named last changes fastest.
Arguments:
- queries: bfloat16 [4, 32, 256, 3072], P('dp', 'frame', 'spatial'), may hold values from -120 to 120
- key_states: bfloat16 [4, 32, 256, 3072], P('dp', 'frame', 'spatial'), may hold values from -6 to 6
- value_states: bfloat16 [4, 32, 256, 3072], P('dp', 'frame', 'spatial'), may hold values from -6 to 6
- out_grad: bfloat16 [4, 32, 256, 3072], P('dp', 'frame', 'spatial'), may hold values from -6 to 6
- head_slopes: float32 [24], replicated, may hold values from 0.05 to 2
- timesteps: int32 [4, 32], P('dp', 'frame'), may hold values from 0 to 999
- stretch_frames: int32 [4, 32], P('dp', 'frame'), may hold values from 3 to 96, as said below
- valid_counts: int32 [4, 32], P('dp', 'frame'), may hold values from 64 to 256, as said below
- mod_weight: float32 [256, 3072], replicated, may hold values from -0.375 to 0.375
Outputs:
- query_grad: bfloat16 [4, 32, 256, 3072], P('dp', 'frame', 'spatial')
- key_grad: bfloat16 [4, 32, 256, 3072], P('dp', 'frame', 'spatial')
- value_grad: bfloat16 [4, 32, 256, 3072], P('dp', 'frame', 'spatial')
- mod_weight_grad: float32 [256, 3072], replicated
The draws below stay inside these ranges and needn't reach their ends.
Inputs may be any that keep to these rules, and one draw needn't show every extreme that they name: `stretch_frames`: strictly increasing along each video's stretches, by 1 to 3 frames a stretch; each video's last stretch stands at frame 3 * 32. `valid_counts`: in every video some stretch is full.
All inputs are finite; a program needn't handle non-finite values.
Results may differ from the reference program's by a relative error of at most 0.02.
Values may be sent and summed in bfloat16 or wider, within the bound.
A program may use at most 128 MiB of HBM per device.

```python
import math
import jax
import jax.numpy as jnp
from jax import lax

HEADS = 24
HEAD = 128
FREQ = 256
SPAN = 3
VIDEOS = 4
STRETCHES = 32
L_STRETCH = 256
WIDTH = 3072


def shared_parts(key):
    full_shape = (VIDEOS, STRETCHES, L_STRETCH, HEADS * HEAD)
    noise = jax.random.normal(jax.random.fold_in(key, 7), full_shape, jnp.float32)
    common = jnp.clip(jax.random.normal(jax.random.fold_in(key, 8), (HEADS * HEAD,), jnp.float32), -2.5, 2.5)
    loudness = jax.random.uniform(jax.random.fold_in(key, 9), (VIDEOS, STRETCHES, 1, 1), jnp.float32, -0.6, 0.6)
    base_keys = jnp.clip(noise + loudness * common, -6.0, 6.0)
    return (base_keys, common)


def draw_key_states(key, part):
    base_keys, common = shared_parts(key)
    return base_keys.astype(jnp.bfloat16)


def draw_queries(key, part):
    base_keys, common = shared_parts(key)
    key = jax.random.fold_in(key, 1)
    full_shape = (VIDEOS, STRETCHES, L_STRETCH, HEADS * HEAD)
    own_values = jnp.clip(jax.random.normal(key, full_shape, jnp.float32), -6.0, 6.0) + common
    plant_strength = 5.0
    planted = plant_strength * base_keys[:, :STRETCHES - SPAN, 2, :]
    own_values = own_values.at[:, SPAN:, 1, :].set(planted)
    return own_values.astype(jnp.bfloat16)


def draw_stretch_frames(key, part):
    key = jax.random.fold_in(key, 4)
    frame_gaps = jax.random.randint(key, (VIDEOS, STRETCHES), 1, 4).astype(jnp.int32)
    frame_gaps = frame_gaps.at[:, 0].set(0)
    gaps_after = jnp.flip(jnp.cumsum(jnp.flip(frame_gaps, axis=1), axis=1), axis=1)
    gaps_after = jnp.concatenate([gaps_after[:, 1:], jnp.zeros((VIDEOS, 1), jnp.int32)], axis=1)
    return (3 * STRETCHES - gaps_after).astype(jnp.int32)


def draw_valid_counts(key, part):
    key = jax.random.fold_in(key, 5)
    first_key, second_key = jax.random.split(key)
    counts = jax.random.randint(first_key, (VIDEOS, STRETCHES), L_STRETCH // 4, L_STRETCH + 1)
    full_stretch = jax.random.randint(second_key, (VIDEOS, 1), 0, STRETCHES)
    return jnp.where(jnp.arange(STRETCHES)[None, :] == full_stretch, L_STRETCH, counts).astype(jnp.int32)


def touch_ends(array, stream_key, smallest, top_value):
    shape = array.shape
    place = [jax.random.randint(jax.random.fold_in(stream_key, axis), (), 0, shape[axis]) for axis in range(len(shape))]
    array = array.at[tuple(place)].set(smallest)
    longest = shape.index(max(shape))
    place[longest] = (place[longest] + 1) % shape[longest]
    return array.at[tuple(place)].set(top_value)


def level_of(key, shape, pieces, low, largest):
    def one(dim, blocks):
        heights = jax.random.uniform(jax.random.fold_in(jax.random.fold_in(key, 6), dim), (blocks,), jnp.float32, low / len(pieces), largest / len(pieces))
        return jnp.repeat(jnp.exp(heights), shape[dim] // blocks).reshape((-1,) + (1,) * (len(shape) - dim - 1))

    level = one(*pieces[0])
    for cut in pieces[1:]:
        level = level * one(*cut)
    return level


def bell_draw(own_key, shape, spread, most, pieces=(), kind=jnp.bfloat16):
    result = jax.random.normal(own_key, shape, jnp.float32) * spread
    if len(pieces) > 0:
        result = level_of(own_key, shape, pieces, -0.22, 0.18) * result
    return jnp.clip(result, min=-most, max=most).astype(kind)


def setup_inputs(seed: int = 0) -> dict:
    key_of = jax.random.split(jax.random.key(seed), 10)
    return {
        "queries": draw_queries(jax.random.fold_in(key_of[9], 71), 0),
        "key_states": draw_key_states(jax.random.fold_in(key_of[9], 71), 0),
        "value_states": bell_draw(key_of[2], (VIDEOS, STRETCHES, L_STRETCH, WIDTH), 1.0, 6.0, ((0, 4), (1, 32), (2, 2))),
        "out_grad": bell_draw(key_of[3], (VIDEOS, STRETCHES, L_STRETCH, WIDTH), 1.0, 6.0, ((0, 4), (1, 32), (2, 2))),
        "head_slopes": jnp.clip(jnp.exp(jax.random.uniform(key_of[4], (HEADS,), jnp.float32, math.log(0.05), math.log(2.0))), 0.05, 2.0),
        "timesteps": touch_ends(jax.random.randint(key_of[5], (VIDEOS, STRETCHES), 0, 1000), jax.random.fold_in(key_of[5], 1), 0, 999).astype(jnp.int32),
        "stretch_frames": draw_stretch_frames(jax.random.fold_in(key_of[9], 71), 0),
        "valid_counts": draw_valid_counts(jax.random.fold_in(key_of[9], 71), 0),
        "mod_weight": bell_draw(key_of[8], (FREQ, WIDTH), FREQ ** -0.5, 0.375, (), jnp.float32),
    }


def timestep_embedding(steps):
    half_count = FREQ // 2
    frequencies = jnp.exp(-math.log(10000.0) * jnp.arange(half_count, dtype=jnp.float32) / half_count)
    angles = steps.astype(jnp.float32)[..., None] * frequencies
    return jnp.concatenate([jnp.cos(angles), jnp.sin(angles)], axis=-1)


def rounded(values):
    return lax.optimization_barrier(values.astype(jnp.bfloat16)).astype(jnp.float32)


def stretch_backward(query_stretch, key_window, value_window, grad_stretch, gate_heads, count_window, frame_window, count_now, frame_now, head_slopes):
    score_scale = HEAD ** -0.5
    query_float = query_stretch.astype(jnp.float32)
    keys_float = key_window.astype(jnp.float32)
    values_float = value_window.astype(jnp.float32)
    grad_float = grad_stretch.astype(jnp.float32)
    scores = jnp.einsum('ihe,jhe->hij', query_float, keys_float) * score_scale
    distance = jnp.repeat((frame_now - frame_window).astype(jnp.float32), L_STRETCH)
    scores = scores - head_slopes[:, None, None] * distance[None, None, :]
    position = jnp.arange((SPAN + 1) * L_STRETCH, dtype=jnp.int32) % L_STRETCH
    visible = position < jnp.repeat(count_window, L_STRETCH)
    scores = jnp.where(visible[None, None, :], scores, -jnp.inf)
    row_max = jnp.max(scores, axis=2, keepdims=True)
    exp_scores = jnp.exp(scores - row_max)
    attn_prob = exp_scores * (1.0 / jnp.sum(exp_scores, axis=2, keepdims=True))
    attn_low = rounded(attn_prob)
    attended = jnp.einsum('hij,jhe->ihe', attn_low, values_float)
    live_rows = (jnp.arange(L_STRETCH, dtype=jnp.int32) < count_now).astype(jnp.float32)[:, None, None]
    gated_grad = rounded(gate_heads[None] * grad_float * live_rows)
    gate_grad = jnp.sum(grad_float * attended * live_rows, axis=0)
    row_delta = jnp.einsum('ihe,ihe->hi', gated_grad, attended)
    grad_prob = jnp.einsum('ihe,jhe->hij', gated_grad, values_float)
    grad_score = rounded(attn_prob * (grad_prob - row_delta[:, :, None]) * score_scale)
    query_part = jnp.einsum('hij,jhe->ihe', grad_score, keys_float)
    key_part = jnp.einsum('hij,ihe->jhe', grad_score, query_float)
    value_part = jnp.einsum('hij,ihe->jhe', attn_low, gated_grad)
    return query_part, key_part, value_part, gate_grad


def reference(queries, key_states, value_states, out_grad, head_slopes, timesteps, stretch_frames, valid_counts, mod_weight):
    emb_rows = timestep_embedding(timesteps).reshape(VIDEOS * STRETCHES, FREQ)
    gates = jnp.dot(emb_rows, mod_weight, precision=lax.Precision.HIGHEST).reshape(VIDEOS, STRETCHES, HEADS, HEAD)
    stretch_shape = (STRETCHES, L_STRETCH, HEADS, HEAD)

    def one_video(video_items):
        query_video, key_video, value_video, grad_video, gate_video, frame_video, count_video = video_items
        query_video = query_video.reshape(stretch_shape)
        grad_video = grad_video.reshape(stretch_shape)
        key_pad = jnp.concatenate([jnp.zeros((SPAN, L_STRETCH, HEADS, HEAD), key_video.dtype), key_video.reshape(stretch_shape)], axis=0)
        value_pad = jnp.concatenate([jnp.zeros((SPAN, L_STRETCH, HEADS, HEAD), value_video.dtype), value_video.reshape(stretch_shape)], axis=0)
        count_pad = jnp.concatenate([jnp.zeros((SPAN,), jnp.int32), count_video.astype(jnp.int32)])
        frame_pad = jnp.concatenate([jnp.zeros((SPAN,), jnp.int32), frame_video.astype(jnp.int32)])

        def stretch_step(accums, stretch_index):
            key_acc, value_acc = accums
            key_window = lax.dynamic_slice_in_dim(key_pad, stretch_index, SPAN + 1, 0).reshape(-1, HEADS, HEAD)
            value_window = lax.dynamic_slice_in_dim(value_pad, stretch_index, SPAN + 1, 0).reshape(-1, HEADS, HEAD)
            count_window = lax.dynamic_slice_in_dim(count_pad, stretch_index, SPAN + 1, 0)
            frame_window = lax.dynamic_slice_in_dim(frame_pad, stretch_index, SPAN + 1, 0)
            query_stretch = lax.dynamic_index_in_dim(query_video, stretch_index, 0, keepdims=False)
            grad_stretch = lax.dynamic_index_in_dim(grad_video, stretch_index, 0, keepdims=False)
            gate_heads = lax.dynamic_index_in_dim(gate_video, stretch_index, 0, keepdims=False)
            count_now = lax.dynamic_index_in_dim(count_video.astype(jnp.int32), stretch_index, 0, keepdims=False)
            frame_now = lax.dynamic_index_in_dim(frame_video.astype(jnp.int32), stretch_index, 0, keepdims=False)
            query_part, key_part, value_part, gate_grad = stretch_backward(query_stretch, key_window, value_window, grad_stretch, gate_heads, count_window, frame_window, count_now, frame_now, head_slopes)
            key_part = key_part.reshape(SPAN + 1, L_STRETCH, HEADS, HEAD)
            value_part = value_part.reshape(SPAN + 1, L_STRETCH, HEADS, HEAD)
            key_acc = lax.dynamic_update_slice_in_dim(key_acc, lax.dynamic_slice_in_dim(key_acc, stretch_index, SPAN + 1, 0) + key_part, stretch_index, 0)
            value_acc = lax.dynamic_update_slice_in_dim(value_acc, lax.dynamic_slice_in_dim(value_acc, stretch_index, SPAN + 1, 0) + value_part, stretch_index, 0)
            return (key_acc, value_acc), (query_part.astype(jnp.bfloat16), gate_grad.reshape(-1))

        zeros_acc = jnp.zeros((STRETCHES + SPAN, L_STRETCH, HEADS, HEAD), jnp.float32)
        (key_acc, value_acc), (query_parts, gate_grads) = lax.scan(stretch_step, (zeros_acc, zeros_acc), jnp.arange(STRETCHES, dtype=jnp.int32))
        return (query_parts.reshape(STRETCHES, L_STRETCH, WIDTH),
                key_acc[SPAN:].astype(jnp.bfloat16).reshape(STRETCHES, L_STRETCH, WIDTH),
                value_acc[SPAN:].astype(jnp.bfloat16).reshape(STRETCHES, L_STRETCH, WIDTH),
                gate_grads)

    query_grad, key_grad, value_grad, gate_grads = lax.map(one_video, (queries, key_states, value_states, out_grad, gates, stretch_frames, valid_counts))
    mod_weight_grad = jnp.dot(emb_rows.T, gate_grads.reshape(VIDEOS * STRETCHES, WIDTH), precision=lax.Precision.HIGHEST)
    return query_grad, key_grad, value_grad, mod_weight_grad
```

```python
import math

import jax
import jax.numpy as jnp
from jax import lax
from jax.sharding import PartitionSpec as P

FREQ = 256
SPAN = 3


def shifted(block, axis, distance):
    devices = range(lax.axis_size(axis))
    route = [(i - distance, i) for i in devices if i - distance in devices]
    return lax.ppermute(block, axis, route)


def timestep_embedding(steps):
    half_count = FREQ // 2
    frequencies = jnp.exp(
        -math.log(10000.0) * jnp.arange(half_count, dtype=jnp.float32) / half_count
    )
    angles = steps.astype(jnp.float32)[..., None] * frequencies
    return jnp.concatenate([jnp.cos(angles), jnp.sin(angles)], axis=-1)


def local(
    queries,
    key_states,
    value_states,
    out_grad,
    head_slopes,
    timesteps,
    stretch_frames,
    valid_counts,
    mod_weight,
):
    tok_rows = queries.shape[2]
    full_width = queries.shape[3]
    head_count = head_slopes.shape[0]
    head_size = full_width // head_count
    spatial_size = lax.axis_size("spatial")
    local_heads = head_count // spatial_size
    channels = local_heads * head_size
    score_scale = head_size ** (-0.5)

    def by_heads(values):
        return values.reshape(tok_rows, head_count, head_size)

    query_local, keys_own, values_own, grad_own = (
        lax.all_to_all(by_heads(queries), "spatial", split_axis=1, concat_axis=0, tiled=True),
        lax.all_to_all(by_heads(key_states), "spatial", split_axis=1, concat_axis=0, tiled=True),
        lax.all_to_all(by_heads(value_states), "spatial", split_axis=1, concat_axis=0, tiled=True),
        lax.all_to_all(by_heads(out_grad), "spatial", split_axis=1, concat_axis=0, tiled=True),
    )
    tokens = query_local.shape[0]
    head_group = lax.axis_index("spatial")
    slopes = lax.dynamic_slice_in_dim(head_slopes, head_group * local_heads, local_heads, 0)
    weight_half = lax.dynamic_slice_in_dim(mod_weight, head_group * channels, channels, 1)
    embedding = timestep_embedding(timesteps[0, 0])
    gate_vec = jnp.dot(embedding[None, :], weight_half, precision=lax.Precision.HIGHEST).reshape(
        local_heads, head_size
    )
    count_now = valid_counts[0, 0]
    frame_now = stretch_frames[0, 0]
    key_list = [keys_own]
    value_list = [values_own]
    count_list = [valid_counts.reshape(1)]
    frame_list = [stretch_frames.reshape(1)]
    for distance in range(1, SPAN + 1):
        arrived = shifted((keys_own, values_own, valid_counts, stretch_frames), "frame", distance)
        key_list.append(arrived[0])
        value_list.append(arrived[1])
        count_list.append(arrived[2].reshape(1))
        frame_list.append(arrived[3].reshape(1))
    key_window = jnp.stack(key_list)
    value_window = jnp.stack(value_list)
    count_window = jnp.concatenate(count_list)
    frame_window = jnp.concatenate(frame_list)
    key_flat = key_window.reshape(-1, local_heads, head_size)
    value_flat = value_window.reshape(-1, local_heads, head_size)
    distance_keys = jnp.repeat((frame_now - frame_window).astype(jnp.float32), tokens)
    visible = (jnp.arange(tokens, dtype=jnp.int32)[None, :] < count_window[:, None]).reshape(-1)
    scores = (
        jnp.einsum("ihe,jhe->hij", query_local, key_flat, preferred_element_type=jnp.float32)
        * score_scale
    )
    scores = scores - slopes[:, None, None] * distance_keys[None, None, :]
    scores = jnp.where(visible[None, None, :], scores, -jnp.inf)
    row_max = jnp.max(scores, axis=2)
    exp_scores = jnp.exp(scores - row_max[:, :, None])
    inv_sum = 1.0 / jnp.sum(exp_scores, axis=2)
    attn_prob = exp_scores * inv_sum[:, :, None]
    attn_low = attn_prob.astype(jnp.bfloat16)
    attended = jnp.einsum("hij,jhe->ihe", attn_low, value_flat, preferred_element_type=jnp.float32)
    live_rows = (jnp.arange(tokens, dtype=jnp.int32) < count_now).astype(jnp.float32)[:, None, None]
    grad_float = grad_own.astype(jnp.float32)
    gated_grad = (gate_vec[None] * grad_float * live_rows).astype(jnp.bfloat16)
    gate_grad = jnp.sum(grad_float * attended * live_rows, axis=0).reshape(-1)
    row_delta = jnp.einsum("ihe,ihe->hi", gated_grad.astype(jnp.float32), attended)
    grad_prob = jnp.einsum(
        "ihe,jhe->hij", gated_grad, value_flat, preferred_element_type=jnp.float32
    )
    grad_score = (attn_prob * (grad_prob - row_delta[:, :, None]) * score_scale).astype(
        jnp.bfloat16
    )
    query_grad = jnp.einsum(
        "hij,jhe->ihe", grad_score, key_flat, preferred_element_type=jnp.float32
    ).astype(jnp.bfloat16)
    key_parts = jnp.einsum(
        "hij,ihe->jhe", grad_score, query_local, preferred_element_type=jnp.float32
    ).reshape(SPAN + 1, tokens, local_heads, head_size)
    value_parts = jnp.einsum(
        "hij,ihe->jhe", attn_low, gated_grad, preferred_element_type=jnp.float32
    ).reshape(SPAN + 1, tokens, local_heads, head_size)
    key_total = key_parts[0]
    value_total = value_parts[0]
    for distance in range(1, SPAN + 1):
        arrived = (
            shifted(key_parts[distance].astype(jnp.bfloat16), "frame", -distance).astype(
                jnp.float32
            ),
            shifted(value_parts[distance].astype(jnp.bfloat16), "frame", -distance).astype(
                jnp.float32
            ),
        )
        key_total = key_total + arrived[0]
        value_total = value_total + arrived[1]
    query_back, key_back, value_back = (
        lax.all_to_all(query_grad, "spatial", split_axis=0, concat_axis=1, tiled=True),
        lax.all_to_all(
            key_total.astype(jnp.bfloat16), "spatial", split_axis=0, concat_axis=1, tiled=True
        ),
        lax.all_to_all(
            value_total.astype(jnp.bfloat16), "spatial", split_axis=0, concat_axis=1, tiled=True
        ),
    )
    out_shape = (1, 1, tok_rows, full_width)
    all_steps = lax.all_gather(timesteps.reshape(1), ("dp", "frame"), axis=0, tiled=True)
    all_embeddings = timestep_embedding(all_steps)
    all_gate_grads = lax.all_gather(
        gate_grad[None, :], ("dp", "frame", "spatial"), axis=0, tiled=True
    ).reshape(all_steps.shape[0], full_width)
    mod_weight_grad = lax.dot_general(
        all_embeddings,
        all_gate_grads,
        (((0,), (0,)), ((), ())),
        precision=lax.Precision.HIGHEST,
        preferred_element_type=jnp.float32,
    )
    return (
        query_back.reshape(out_shape),
        key_back.reshape(out_shape),
        value_back.reshape(out_shape),
        mod_weight_grad,
    )


def solution(mesh):
    in_specs = (
        P("dp", "frame", "spatial", None),
        P("dp", "frame", "spatial", None),
        P("dp", "frame", "spatial", None),
        P("dp", "frame", "spatial", None),
        P(),
        P("dp", "frame"),
        P("dp", "frame"),
        P("dp", "frame"),
        P(),
    )
    out_specs = (
        P("dp", "frame", "spatial", None),
        P("dp", "frame", "spatial", None),
        P("dp", "frame", "spatial", None),
        P(),
    )
    return jax.shard_map(local, mesh=mesh, in_specs=in_specs, out_specs=out_specs, check_vma=False)
```

```python
import math

import jax
import jax.numpy as jnp
import numpy as np
from jax import lax
from jax.experimental import pallas as pl
from jax.experimental.pallas import tpu as pltpu
from jax.sharding import PartitionSpec as P

MESH = pl.DeviceIdType.MESH
F32 = jnp.float32
BF16 = jnp.bfloat16
HIGHEST = lax.Precision.HIGHEST

NX, NZ, NY, NS = 4, 8, 4, 2
GROUP = NY * NS
SPAN = 3
SLOTS = SPAN + NY
TOK = 256
PART = TOK // NS
HEAD = 128
HEADS = 24
MINE = HEADS // GROUP
CHUNK = MINE * HEAD
WIDTH = HEADS * HEAD
FREQ = 256
SCALE = HEAD ** (-0.5)
LOG2E = math.log2(math.e)
HIDDEN = -1e30
NT = (((1,), (1,)), ((), ()))
TN = (((0,), (0,)), ((), ()))


def dot(a, b, dims=(((1,), (0,)), ((), ()))):
    return lax.dot_general(a, b, dims, preferred_element_type=F32)


def main_kernel(
    freq_ref, slope_ref, step_ref, frame_ref, count_ref, weight_ref,
    q_in, k_in, v_in, g_in,
    dq_out, dk_out, dv_out, mod_out,
    qb, kb, vb, gb, kt, vt, weight, meta, times, rows_t, gate, emb_hi, emb_lo, bias,
    x_s, p_s, d_s, dk_acc, dv_acc, dq_s, dk_s, dv_s, halo_s, halo_r, dgate, terms,
    in_recv, in_send, z_recv, z_send, h_recv, h_send, o_recv, o_send, o_loc,
    m_recv, m_send, t_recv, t_send, w_sem,
):
    x = lax.axis_index("dp")
    frame = lax.axis_index("frame")
    s = lax.axis_index("spatial")
    z = frame // NY
    y = frame % NY
    p = y * NS + s

    def group_dev(k):
        other = (p + k) % GROUP
        return (x, z * NY + other // NS, other % NS), other

    def y_dev(k):
        return (x, z * NY + (y + k) % NY, s)

    def z_dev(k):
        return (x, ((z + k) % NZ) * NY + y, s)

    def x_dev(k):
        return ((x + k) % NX, frame, s)

    def loop(low, high, body):
        def step(k, carry):
            body(k)
            return carry

        lax.fori_loop(low, high, step, 0)

    def send(src, dst, send_sem, recv_sem, device):
        pltpu.make_async_remote_copy(
            src_ref=src, dst_ref=dst, send_sem=send_sem, recv_sem=recv_sem,
            device_id=device, device_id_type=MESH,
        ).start()

    def wait(ref, sem):
        pltpu.make_async_copy(ref, ref, sem).wait()

    barrier = pltpu.get_barrier_semaphore()

    def greet(device):
        pl.semaphore_signal(barrier, inc=1, device_id=device, device_id_type=MESH)

    loop(1, GROUP, lambda k: greet(group_dev(k)[0]))
    loop(1, NZ, lambda k: greet(z_dev(k)))
    loop(1, NX, lambda k: greet(x_dev(k)))

    weight_copy = pltpu.make_async_copy(
        weight_ref.at[:, pl.ds(pl.multiple_of(p * CHUNK, HEAD), CHUNK)], weight, w_sem
    )
    weight_copy.start()
    line = lax.broadcasted_iota(jnp.int32, (8, HEAD), 0)
    meta[y] = jnp.where(
        line == 0, count_ref[0], jnp.where(line == 1, frame_ref[0], step_ref[0])
    )
    arrays = ((k_in, kb, SPAN), (v_in, vb, SPAN), (q_in, qb, 0), (g_in, gb, 0))

    def column(owner, h):
        return pl.ds(pl.multiple_of(owner * CHUNK + h * HEAD, HEAD), HEAD)

    def own_part(a, h):
        src, dst, first = arrays[a]
        pltpu.make_async_copy(
            src.at[:, column(p, h)], dst.at[h, first + y, pl.ds(s * PART, PART)], in_recv.at[a, h]
        ).start()

    for a in range(4):
        loop(0, MINE, lambda h, a=a: own_part(a, h))

    pl.semaphore_wait(barrier, GROUP - 1 + NZ - 1 + NX - 1)

    loop(1, NY, lambda k: send(meta.at[y], meta.at[y], m_send.at[0], m_recv.at[0], y_dev(k)))

    def send_part(a, h, k):
        src, dst, first = arrays[a]
        device, owner = group_dev(k)
        send(
            src.at[:, column(owner, h)], dst.at[h, first + y, pl.ds(s * PART, PART)],
            in_send.at[a, h], in_recv.at[a, h], device,
        )

    def send_pair(first, h):
        for a in (first, first + 1):
            loop(1, GROUP, lambda k, a=a: send_part(a, h, k))

    loop(0, MINE, lambda h: send_pair(0, h))
    loop(0, MINE, lambda h: send_pair(2, h))

    wait(meta.at[pl.ds(0, NY - 1)], m_recv.at[0])
    times[x, z] = meta[...]
    loop(1, NZ, lambda k: send(meta, times.at[x, z], m_send.at[1], m_recv.at[1], z_dev(k)))
    rows_t[...] = jnp.zeros_like(rows_t)
    for i in range(NY):
        rows_t[i : i + 1, :] = meta[i, 2:3, :].astype(F32)
    angles = rows_t[0:8, :] * freq_ref[...]
    emb = jnp.concatenate([jnp.cos(angles), jnp.sin(angles)], axis=1)
    weight_copy.wait()
    gates = lax.dot_general(
        emb, weight[...], (((1,), (0,)), ((), ())), precision=HIGHEST, preferred_element_type=F32
    )
    for h in range(MINE):
        gate[h] = gates[:, h * HEAD : (h + 1) * HEAD]

    def pass_on(h):
        wait(kb.at[h, pl.ds(SPAN, NY)], in_recv.at[0, h])
        send(
            kb.at[h, pl.ds(NY, SPAN)], kb.at[h, pl.ds(0, SPAN)],
            z_send.at[0, h], z_recv.at[0, h], z_dev(1),
        )
        wait(vb.at[h, pl.ds(SPAN, NY)], in_recv.at[1, h])
        send(
            vb.at[h, pl.ds(NY, SPAN)], vb.at[h, pl.ds(0, SPAN)],
            z_send.at[1, h], z_recv.at[1, h], z_dev(1),
        )

    loop(0, 1, pass_on)
    wait(times.at[0, pl.ds(0, NZ - 1)], m_recv.at[1])
    loop(1, NX, lambda k: send(times.at[x], times.at[x], m_send.at[2], m_recv.at[2], x_dev(k)))
    loop(1, MINE, pass_on)

    wait(times.at[pl.ds(0, NX - 1)], m_recv.at[2])

    def take_row(n):
        for i in range(NY):
            rows_t[pl.ds(n * NY + i, 1), :] = times[n // NZ, n % NZ, i, 2:3, :].astype(F32)

    loop(0, NX * NZ, take_row)

    def features(n):
        angle = rows_t[pl.ds(pl.multiple_of(n * 8, 8), 8), :] * freq_ref[...]
        both = jnp.concatenate([jnp.cos(angle), jnp.sin(angle)], axis=1)
        for half in range(2):
            four = both[half * NY : (half + 1) * NY]
            tile = jnp.concatenate([four, four, four, four], axis=0)
            high = tile.astype(BF16)
            at = pl.ds(pl.multiple_of(n * 32 + half * 16, 16), 16)
            emb_hi[at, :] = high
            emb_lo[at, :] = (tile - high.astype(F32)).astype(BF16)

    loop(0, NX * NZ // 2, features)

    token = lax.broadcasted_iota(jnp.int32, (TOK, HEAD), 0)
    z_before = (z + NZ - 1) % NZ
    has_before = jnp.minimum(z, 1)
    base = times[x, z, NY - 1, 1:2, :]

    def head(h):
        wait(kb.at[h, pl.ds(0, SPAN)], z_recv.at[0, h])
        wait(vb.at[h, pl.ds(0, SPAN)], z_recv.at[1, h])
        kt[...] = kb[h].reshape(SLOTS * TOK, HEAD).T
        vt[...] = vb[h].reshape(SLOTS * TOK, HEAD).T
        slope = slope_ref[p * MINE + h] * LOG2E
        for slot in range(SLOTS):
            if slot < SPAN:
                count = times[x, z_before, slot + 1, 0:1, :] * has_before
                place = times[x, z_before, slot + 1, 1:2, :]
            else:
                count = times[x, z, slot - SPAN, 0:1, :]
                place = times[x, z, slot - SPAN, 1:2, :]
            shift = (place - base).astype(F32) * slope
            bias[slot] = jnp.where(token < count, shift, HIDDEN)
        dk_acc[h] = jnp.zeros((SLOTS, TOK, HEAD), F32)
        dv_acc[h] = jnp.zeros((SLOTS, TOK, HEAD), F32)
        wait(qb.at[h], in_recv.at[2, h])
        wait(gb.at[h], in_recv.at[3, h])

        def stretch(i):
            q = qb[h, i]
            live = token < times[x, z, i, 0:1, :]
            grad = jnp.where(live, gb[h, i].astype(F32), 0.0)
            go = (gate[h, pl.ds(i, 1), :] * grad).astype(BF16)
            top = jnp.full((1, TOK), HIDDEN, F32)
            for k in range(SPAN + 1):
                one = bias[i + k]
                value = dot(kb[h, i + k], q, NT) * (SCALE * LOG2E) + jnp.concatenate([one, one], axis=1)
                x_s[k] = value
                top = jnp.maximum(top, jnp.max(value, axis=0, keepdims=True))
            total = jnp.zeros((1, TOK), F32)
            for k in range(SPAN + 1):
                value = jnp.exp2(x_s[k] - top)
                x_s[k] = value
                total = total + jnp.sum(value, axis=0, keepdims=True)
            inverse = 1.0 / total
            for k in range(SPAN + 1):
                value = x_s[k] * inverse
                x_s[k] = value
                p_s[k] = value.astype(BF16)
            window = pl.ds(pl.multiple_of(i * TOK, TOK), (SPAN + 1) * TOK)
            out_t = dot(vt[:, window], p_s[...].reshape((SPAN + 1) * TOK, TOK))
            delta = jnp.sum(go.astype(F32).T * out_t, axis=0, keepdims=True)
            dgate[pl.ds(h * NY + i, 1), :] = jnp.sum(grad * out_t.T, axis=0, keepdims=True)
            for k in range(SPAN + 1):
                d_s[k] = (x_s[k] * (dot(vb[h, i + k], go, NT) - delta) * SCALE).astype(BF16)
            dq_s[h, i] = dot(kt[:, window], d_s[...].reshape((SPAN + 1) * TOK, TOK)).T.astype(BF16)
            for k in range(SPAN + 1):
                dk_acc[h, i + k] += dot(d_s[k], q)
                dv_acc[h, i + k] += dot(p_s[k], go)

        loop(0, NY, stretch)
        halo_s[h, 0] = dk_acc[h, 0:SPAN].astype(BF16)
        halo_s[h, 1] = dv_acc[h, 0:SPAN].astype(BF16)
        send(halo_s.at[h], halo_r.at[h], h_send.at[h], h_recv.at[h], z_dev(NZ - 1))

    def give_back(a, staged, out, h):
        def one(k):
            device, owner = group_dev(k)
            send(
                staged.at[h, owner // NS, pl.ds((owner % NS) * PART, PART)], out.at[:, column(p, h)],
                o_send.at[a], o_recv.at[a], device,
            )

        loop(1, GROUP, one)
        pltpu.make_async_copy(
            staged.at[h, y, pl.ds(s * PART, PART)], out.at[:, column(p, h)], o_loc.at[a]
        ).start()

    has_after = jnp.minimum(NZ - 1 - z, 1).astype(F32)

    def finish(h):
        wait(halo_r.at[h], h_recv.at[h])
        for n, (acc, staged) in enumerate(((dk_acc, dk_s), (dv_acc, dv_s))):
            staged[h, 0] = acc[h, SPAN].astype(BF16)
            for i in range(1, NY):
                staged[h, i] = (
                    acc[h, SPAN + i] + halo_r[h, n, i - 1].astype(F32) * has_after
                ).astype(BF16)
        give_back(1, dk_s, dk_out, h)
        give_back(2, dv_s, dv_out, h)

    dgate[...] = jnp.zeros_like(dgate)
    for h in range(MINE):
        head(h)
        give_back(0, dq_s, dq_out, h)
        if h > 0:
            finish(h - 1)

    terms[s, x, z, y] = dgate[...].astype(BF16)
    mine = terms.at[s, x, z, y]
    loop(1, NY, lambda k: send(mine, mine, t_send.at[0], t_recv.at[0], y_dev(k)))
    wait(terms.at[0, 0, 0, pl.ds(0, NY - 1)], t_recv.at[0])
    along_y = terms.at[s, x, z]
    loop(1, NZ, lambda k: send(along_y, along_y, t_send.at[1], t_recv.at[1], z_dev(k)))
    wait(terms.at[0, 0, pl.ds(0, NZ - 1)], t_recv.at[1])
    along_z = terms.at[s, x]
    loop(1, NX, lambda k: send(along_z, along_z, t_send.at[2], t_recv.at[2], x_dev(k)))
    finish(MINE - 1)
    wait(terms.at[0, pl.ds(0, NX - 1)], t_recv.at[2])
    along_x = terms.at[s]
    send(along_x, along_x, t_send.at[3], t_recv.at[3], (x, frame, 1 - s))
    wait(terms.at[0], t_recv.at[3])

    row = lax.broadcasted_iota(jnp.int32, (16, HEAD), 0)
    for h in range(MINE):
        keep = jnp.where(row // NY == h, 1.0, 0.0).astype(BF16)
        for other in range(NY):
            cores = [
                (terms[core, :, :, other] * keep).reshape(NX * NZ * 16, HEAD) for core in range(NS)
            ]
            both = jnp.concatenate(cores, axis=1)
            part = dot(emb_hi[...], both, TN) + dot(emb_lo[...], both, TN)
            for core in range(NS):
                at = (other * NS + core) * CHUNK + h * HEAD
                mod_out[:, at : at + HEAD] = part[:, core * HEAD : (core + 1) * HEAD]

    outs = (dq_out, dk_out, dv_out)
    arrived = pl.ds(0, (GROUP - 1) * CHUNK)
    for a in range(3):
        wait(outs[a].at[:, arrived], o_recv.at[a])
        wait(outs[a].at[:, arrived], o_send.at[a])
        wait(outs[a].at[:, pl.ds(0, CHUNK)], o_loc.at[a])
    for a in range(4):
        for h in range(MINE):
            wait(q_in.at[:, pl.ds(0, (GROUP - 1) * HEAD)], in_send.at[a, h])
    for h in range(MINE):
        wait(kb.at[h, pl.ds(0, SPAN)], z_send.at[0, h])
        wait(vb.at[h, pl.ds(0, SPAN)], z_send.at[1, h])
        wait(halo_s.at[h], h_send.at[h])
    wait(meta.at[pl.ds(0, NY - 1)], m_send.at[0])
    wait(times.at[0, pl.ds(0, NZ - 1)], m_send.at[1])
    wait(times.at[pl.ds(0, NX - 1)], m_send.at[2])
    wait(terms.at[0, 0, 0, pl.ds(0, NY - 1)], t_send.at[0])
    wait(terms.at[0, 0, pl.ds(0, NZ - 1)], t_send.at[1])
    wait(terms.at[0, pl.ds(0, NX - 1)], t_send.at[2])
    wait(terms.at[0], t_send.at[3])


def local(
    queries, key_states, value_states, out_grad, head_slopes, timesteps, stretch_frames,
    valid_counts, mod_weight,
):
    half = FREQ // 2
    freq = jnp.asarray(
        np.exp(-math.log(10000.0) * np.arange(half) / half).astype(np.float32)[None, :]
    )
    flat = (PART, WIDTH)
    anywhere = pl.BlockSpec(memory_space=pl.ANY)
    smem = pl.BlockSpec(memory_space=pltpu.SMEM)
    vmem = pl.BlockSpec(memory_space=pltpu.VMEM)
    dma = pltpu.SemaphoreType.DMA
    grad = jax.ShapeDtypeStruct(flat, BF16)
    dq, dk, dv, mod = pl.pallas_call(
        main_kernel,
        name="attention_backward",
        out_shape=(grad, grad, grad, jax.ShapeDtypeStruct((FREQ, WIDTH), F32)),
        in_specs=[vmem, smem, smem, smem, smem] + [anywhere] * 5,
        out_specs=(anywhere, anywhere, anywhere, vmem),
        scratch_shapes=[
            pltpu.VMEM((MINE, NY, TOK, HEAD), BF16),
            pltpu.VMEM((MINE, SLOTS, TOK, HEAD), BF16),
            pltpu.VMEM((MINE, SLOTS, TOK, HEAD), BF16),
            pltpu.VMEM((MINE, NY, TOK, HEAD), BF16),
            pltpu.VMEM((HEAD, SLOTS * TOK), BF16),
            pltpu.VMEM((HEAD, SLOTS * TOK), BF16),
            pltpu.VMEM((FREQ, CHUNK), F32),
            pltpu.VMEM((NY, 8, HEAD), jnp.int32),
            pltpu.VMEM((NX, NZ, NY, 8, HEAD), jnp.int32),
            pltpu.VMEM((NX * NZ * NY, HEAD), F32),
            pltpu.VMEM((MINE, 8, HEAD), F32),
            pltpu.VMEM((NX * NZ * 16, FREQ), BF16),
            pltpu.VMEM((NX * NZ * 16, FREQ), BF16),
            pltpu.VMEM((SLOTS, TOK, HEAD), F32),
            pltpu.VMEM((SPAN + 1, TOK, TOK), F32),
            pltpu.VMEM((SPAN + 1, TOK, TOK), BF16),
            pltpu.VMEM((SPAN + 1, TOK, TOK), BF16),
            pltpu.VMEM((MINE, SLOTS, TOK, HEAD), F32),
            pltpu.VMEM((MINE, SLOTS, TOK, HEAD), F32),
            pltpu.VMEM((MINE, NY, TOK, HEAD), BF16),
            pltpu.VMEM((MINE, NY, TOK, HEAD), BF16),
            pltpu.VMEM((MINE, NY, TOK, HEAD), BF16),
            pltpu.VMEM((MINE, 2, SPAN, TOK, HEAD), BF16),
            pltpu.VMEM((MINE, 2, SPAN, TOK, HEAD), BF16),
            pltpu.VMEM((16, HEAD), F32),
            pltpu.VMEM((NS, NX, NZ, NY, 16, HEAD), BF16),
            dma((4, MINE)), dma((4, MINE)),
            dma((2, MINE)), dma((2, MINE)),
            dma((MINE,)), dma((MINE,)),
            dma((3,)), dma((3,)), dma((3,)),
            dma((3,)), dma((3,)),
            dma((4,)), dma((4,)),
            dma,
        ],
        compiler_params=pltpu.CompilerParams(
            collective_id=0, has_side_effects=True, vmem_limit_bytes=48 * 2**20
        ),
    )(
        freq, head_slopes, timesteps.reshape(1), stretch_frames.reshape(1), valid_counts.reshape(1),
        mod_weight, queries.reshape(flat), key_states.reshape(flat), value_states.reshape(flat),
        out_grad.reshape(flat),
    )
    whole = (1, 1, PART, WIDTH)
    return dq.reshape(whole), dk.reshape(whole), dv.reshape(whole), mod


def solution(mesh):
    tokens = P("dp", "frame", "spatial", None)
    each = P("dp", "frame")
    return jax.shard_map(
        local,
        mesh=mesh,
        in_specs=(tokens, tokens, tokens, tokens, P(), each, each, each, P()),
        out_specs=(tokens, tokens, tokens, P()),
        check_vma=False,
    )
```

```python
import math

import jax
import jax.numpy as jnp
from jax import lax
from jax.experimental import pallas as pl
from jax.experimental.pallas import tpu as pltpu
from jax.sharding import PartitionSpec as P

MESH = pl.DeviceIdType.MESH
F32 = jnp.float32
BF16 = jnp.bfloat16
HIGHEST = lax.Precision.HIGHEST

NX, NZ, NY, NS = 4, 8, 4, 2
GROUP = NY * NS
SPAN = 3
SLOTS = SPAN + NY
TOK = 256
PART = TOK // NS
HEAD = 128
HEADS = 24
MINE = HEADS // GROUP
CHUNK = MINE * HEAD
WIDTH = HEADS * HEAD
FREQ = 256
SCALE = HEAD ** (-0.5)
LOG2E = math.log2(math.e)
HIDDEN = -1e30
NT = (((1,), (1,)), ((), ()))
TN = (((0,), (0,)), ((), ()))


def dot(a, b, dims=(((1,), (0,)), ((), ()))):
    return lax.dot_general(a, b, dims, preferred_element_type=F32)


def main_kernel(
    slope_ref, step_ref, frame_ref, count_ref, weight_ref,
    q_in, k_in, v_in, g_in,
    dq_out, dk_out, dv_out, mod_out,
    qb, kb, vb, gb, kt, vt, weight, meta, times, rows_t, gate, emb, emb_hi, emb_lo, bias,
    x_s, p_s, d_s, dk_acc, dv_acc, dq_s, dk_s, dv_s, halo_s, halo_r, dgate, rows_y, terms,
    in_recv, in_send, z_recv, z_send, h_recv, h_send, o_recv, o_send, o_loc,
    m_recv, m_send, t_recv, t_send, w_sem,
):
    x = lax.axis_index("dp")
    frame = lax.axis_index("frame")
    s = lax.axis_index("spatial")
    z = frame // NY
    y = frame % NY
    p = y * NS + s

    def group_dev(k):
        other = (p + k) % GROUP
        return (x, z * NY + other // NS, other % NS), other

    def y_dev(k):
        return (x, z * NY + (y + k) % NY, s)

    def z_dev(k):
        return (x, ((z + k) % NZ) * NY + y, s)

    def x_dev(k):
        return ((x + k) % NX, frame, s)

    def loop(low, high, body):
        def step(k, carry):
            body(k)
            return carry

        lax.fori_loop(low, high, step, 0)

    def send(src, dst, send_sem, recv_sem, device):
        pltpu.make_async_remote_copy(
            src_ref=src, dst_ref=dst, send_sem=send_sem, recv_sem=recv_sem,
            device_id=device, device_id_type=MESH,
        ).start()

    def wait(ref, sem):
        pltpu.make_async_copy(ref, ref, sem).wait()

    barrier = pltpu.get_barrier_semaphore()

    def greet(device):
        pl.semaphore_signal(barrier, inc=1, device_id=device, device_id_type=MESH)

    loop(1, GROUP, lambda k: greet(group_dev(k)[0]))
    loop(1, NZ, lambda k: greet(z_dev(k)))
    loop(1, NX, lambda k: greet(x_dev(k)))

    weight_copy = pltpu.make_async_copy(
        weight_ref.at[:, pl.ds(pl.multiple_of(p * CHUNK, HEAD), CHUNK)], weight, w_sem
    )
    weight_copy.start()
    line = lax.broadcasted_iota(jnp.int32, (8, HEAD), 0)
    steps = lax.broadcasted_iota(jnp.int32, (1, HEAD), 1).astype(F32)
    freq = jnp.exp(steps * (-math.log(10000.0) / (FREQ // 2)))
    meta[y] = jnp.where(
        line == 0, count_ref[0, 0], jnp.where(line == 1, frame_ref[0, 0], step_ref[0, 0])
    )
    arrays = ((k_in, kb, SPAN), (v_in, vb, SPAN), (q_in, qb, 0), (g_in, gb, 0))

    def column(owner, h):
        return pl.ds(pl.multiple_of(owner * CHUNK + h * HEAD, HEAD), HEAD)

    def own_part(a, h):
        src, dst, first = arrays[a]
        pltpu.make_async_copy(
            src.at[:, column(p, h)], dst.at[h, first + y, pl.ds(s * PART, PART)], in_recv.at[a, h]
        ).start()

    for a in range(4):
        loop(0, MINE, lambda h, a=a: own_part(a, h))

    pl.semaphore_wait(barrier, GROUP - 1 + NZ - 1 + NX - 1)

    loop(1, NY, lambda k: send(meta.at[y], meta.at[y], m_send.at[0], m_recv.at[0], y_dev(k)))

    def send_part(a, h, k):
        src, dst, first = arrays[a]
        device, owner = group_dev(k)
        send(
            src.at[:, column(owner, h)], dst.at[h, first + y, pl.ds(s * PART, PART)],
            in_send.at[a, h], in_recv.at[a, h], device,
        )

    def send_pair(first, h):
        for a in (first, first + 1):
            loop(1, GROUP, lambda k, a=a: send_part(a, h, k))

    send_pair(0, 0)
    send_pair(2, 0)
    send_pair(0, 1)

    wait(meta.at[pl.ds(0, NY - 1)], m_recv.at[0])
    times[x, z] = meta[...]
    loop(1, NZ, lambda k: send(meta, times.at[x, z], m_send.at[1], m_recv.at[1], z_dev(k)))
    rows_t[...] = jnp.zeros_like(rows_t)
    for i in range(NY):
        rows_t[i : i + 1, :] = meta[i, 2:3, :].astype(F32)
    angles = rows_t[0:8, :] * freq
    own_emb = jnp.concatenate([jnp.cos(angles), jnp.sin(angles)], axis=1)
    weight_copy.wait()
    gates = lax.dot_general(
        own_emb, weight[...], (((1,), (0,)), ((), ())), precision=HIGHEST, preferred_element_type=F32
    )
    for h in range(MINE):
        gate[h] = gates[:, h * HEAD : (h + 1) * HEAD]

    def pass_on(h):
        wait(kb.at[h, pl.ds(SPAN, NY)], in_recv.at[0, h])
        send(
            kb.at[h, pl.ds(NY, SPAN)], kb.at[h, pl.ds(0, SPAN)],
            z_send.at[0, h], z_recv.at[0, h], z_dev(1),
        )
        wait(vb.at[h, pl.ds(SPAN, NY)], in_recv.at[1, h])
        send(
            vb.at[h, pl.ds(NY, SPAN)], vb.at[h, pl.ds(0, SPAN)],
            z_send.at[1, h], z_recv.at[1, h], z_dev(1),
        )

    def arrive(h):
        wait(qb.at[h], in_recv.at[2, h])
        wait(gb.at[h], in_recv.at[3, h])

    pass_on(0)
    send_pair(0, 2)
    wait(times.at[0, pl.ds(0, NZ - 1)], m_recv.at[1])
    loop(1, NX, lambda k: send(times.at[x], times.at[x], m_send.at[2], m_recv.at[2], x_dev(k)))
    arrive(0)
    send_pair(2, 1)
    pass_on(1)
    send_pair(2, 2)

    wait(times.at[pl.ds(0, NX - 1)], m_recv.at[2])

    def take_row(n):
        for i in range(NY):
            rows_t[pl.ds(n * NY + i, 1), :] = times[n // NZ, n % NZ, i, 2:3, :].astype(F32)

    loop(0, NX * NZ, take_row)

    def features(n):
        angle = rows_t[pl.ds(pl.multiple_of(n * 8, 8), 8), :] * freq
        both = jnp.concatenate([jnp.cos(angle), jnp.sin(angle)], axis=1)
        for half in range(2):
            four = both[half * NY : (half + 1) * NY]
            tile = jnp.concatenate([four, four, four, four], axis=0)
            emb[pl.ds(pl.multiple_of(n * 32 + half * 16, 16), 16), :] = tile

    loop(0, NX * NZ // 2, features)
    turned = emb[...].T
    emb_hi[...] = turned.astype(BF16)
    emb_lo[...] = (turned - turned.astype(BF16).astype(F32)).astype(BF16)

    token = lax.broadcasted_iota(jnp.int32, (TOK, HEAD), 0)
    z_before = (z + NZ - 1) % NZ
    has_before = jnp.minimum(z, 1)
    base = times[x, z, NY - 1, 1:2, :]

    def head(h):
        wait(kb.at[h, pl.ds(0, SPAN)], z_recv.at[0, h])
        wait(vb.at[h, pl.ds(0, SPAN)], z_recv.at[1, h])
        kt[...] = kb[h].reshape(SLOTS * TOK, HEAD).T
        vt[...] = vb[h].reshape(SLOTS * TOK, HEAD).T
        slope = slope_ref[p * MINE + h] * LOG2E
        for slot in range(SLOTS):
            if slot < SPAN:
                count = times[x, z_before, slot + 1, 0:1, :] * has_before
                place = times[x, z_before, slot + 1, 1:2, :]
            else:
                count = times[x, z, slot - SPAN, 0:1, :]
                place = times[x, z, slot - SPAN, 1:2, :]
            shift = (place - base).astype(F32) * slope
            bias[slot] = jnp.where(token < count, shift, HIDDEN)
        dk_acc[h] = jnp.zeros((SLOTS, TOK, HEAD), F32)
        dv_acc[h] = jnp.zeros((SLOTS, TOK, HEAD), F32)

        def stretch(i):
            q = qb[h, i]
            live = token < times[x, z, i, 0:1, :]
            grad = jnp.where(live, gb[h, i].astype(F32), 0.0)
            go = (gate[h, pl.ds(i, 1), :] * grad).astype(BF16)
            top = jnp.full((1, TOK), HIDDEN, F32)
            for k in range(SPAN + 1):
                one = bias[i + k]
                value = dot(kb[h, i + k], q, NT) * (SCALE * LOG2E) + jnp.concatenate([one, one], axis=1)
                x_s[k] = value
                top = jnp.maximum(top, jnp.max(value, axis=0, keepdims=True))
            total = jnp.zeros((1, TOK), F32)
            for k in range(SPAN + 1):
                value = jnp.exp2(x_s[k] - top)
                x_s[k] = value
                total = total + jnp.sum(value, axis=0, keepdims=True)
            inverse = 1.0 / total
            for k in range(SPAN + 1):
                value = x_s[k] * inverse
                x_s[k] = value
                p_s[k] = value.astype(BF16)
            window = pl.ds(pl.multiple_of(i * TOK, TOK), (SPAN + 1) * TOK)
            out_t = dot(vt[:, window], p_s[...].reshape((SPAN + 1) * TOK, TOK))
            delta = jnp.sum(go.astype(F32).T * out_t, axis=0, keepdims=True)
            dgate[h, pl.ds(y * NY + i, 1), :] = jnp.sum(grad * out_t.T, axis=0, keepdims=True)
            for k in range(SPAN + 1):
                d_s[k] = (x_s[k] * (dot(vb[h, i + k], go, NT) - delta) * SCALE).astype(BF16)
            dq_s[h, i] = dot(kt[:, window], d_s[...].reshape((SPAN + 1) * TOK, TOK)).T.astype(BF16)
            for k in range(SPAN + 1):
                dk_acc[h, i + k] += dot(d_s[k], q)
                dv_acc[h, i + k] += dot(p_s[k], go)

        loop(0, SPAN, stretch)
        halo_s[h, 0] = dk_acc[h, 0:SPAN].astype(BF16)
        halo_s[h, 1] = dv_acc[h, 0:SPAN].astype(BF16)
        send(halo_s.at[h], halo_r.at[h], h_send.at[h], h_recv.at[h], z_dev(NZ - 1))
        stretch(SPAN)

    def give_back(a, staged, out, h):
        def one(k):
            device, owner = group_dev(k)
            send(
                staged.at[h, owner // NS, pl.ds((owner % NS) * PART, PART)], out.at[:, column(p, h)],
                o_send.at[a], o_recv.at[a], device,
            )

        loop(1, GROUP, one)
        pltpu.make_async_copy(
            staged.at[h, y, pl.ds(s * PART, PART)], out.at[:, column(p, h)], o_loc.at[a]
        ).start()

    has_after = jnp.minimum(NZ - 1 - z, 1).astype(F32)

    def finish(h):
        wait(halo_r.at[h], h_recv.at[h])
        for n, (acc, staged) in enumerate(((dk_acc, dk_s), (dv_acc, dv_s))):
            staged[h, 0] = acc[h, SPAN].astype(BF16)
            for i in range(1, NY):
                staged[h, i] = (
                    acc[h, SPAN + i] + halo_r[h, n, i - 1].astype(F32) * has_after
                ).astype(BF16)
        give_back(1, dk_s, dk_out, h)
        give_back(2, dv_s, dv_out, h)

    dgate[...] = jnp.zeros_like(dgate)
    def along_y(h):
        rows_y[h, y] = dgate[h].astype(BF16)
        mine = rows_y.at[h, y]
        loop(1, NY, lambda k: send(mine, mine, t_send.at[0, h], t_recv.at[0, h], y_dev(k)))

    def along_z(h):
        wait(rows_y.at[h, pl.ds(0, NY - 1)], t_recv.at[0, h])
        terms[h, s, x, z] = jnp.sum(rows_y[h].astype(F32), axis=0).astype(BF16)
        mine = terms.at[h, s, x, z]
        loop(1, NZ, lambda k: send(mine, mine, t_send.at[1, h], t_recv.at[1, h], z_dev(k)))

    def along_x(h):
        wait(terms.at[h, 0, 0, pl.ds(0, NZ - 1)], t_recv.at[1, h])
        mine = terms.at[h, s, x]
        loop(1, NX, lambda k: send(mine, mine, t_send.at[2, h], t_recv.at[2, h], x_dev(k)))

    def to_core(h):
        wait(terms.at[h, 0, pl.ds(0, NX - 1)], t_recv.at[2, h])
        send(terms.at[h, s], terms.at[h, s], t_send.at[3, h], t_recv.at[3, h], (x, frame, 1 - s))

    row = lax.broadcasted_iota(jnp.int32, (16, HEAD), 0)

    def contract(h):
        wait(terms.at[h, 0], t_recv.at[3, h])
        for other in range(NY):
            keep = jnp.where(row // NY == other, 1.0, 0.0).astype(BF16)
            cores = [(terms[h, core] * keep).reshape(NX * NZ * 16, HEAD) for core in range(NS)]
            both = jnp.concatenate(cores, axis=1)
            part = dot(emb_hi[...], both) + dot(emb_lo[...], both)
            for core in range(NS):
                at = (other * NS + core) * CHUNK + h * HEAD
                mod_out[:, at : at + HEAD] = part[:, core * HEAD : (core + 1) * HEAD]

    head(0)
    along_y(0)
    give_back(0, dq_s, dq_out, 0)
    pass_on(2)
    arrive(1)
    head(1)
    along_y(1)
    give_back(0, dq_s, dq_out, 1)
    arrive(2)
    head(2)
    along_y(2)
    along_z(0)
    give_back(0, dq_s, dq_out, 2)
    finish(0)
    finish(1)
    along_z(1)
    along_x(0)
    along_z(2)
    along_x(1)
    to_core(0)
    finish(2)
    along_x(2)
    to_core(1)
    contract(0)
    to_core(2)
    contract(1)
    contract(2)

    outs = (dq_out, dk_out, dv_out)
    arrived = pl.ds(0, (GROUP - 1) * CHUNK)
    for a in range(3):
        wait(outs[a].at[:, arrived], o_recv.at[a])
        wait(outs[a].at[:, arrived], o_send.at[a])
        wait(outs[a].at[:, pl.ds(0, CHUNK)], o_loc.at[a])
    for a in range(4):
        for h in range(MINE):
            wait(q_in.at[:, pl.ds(0, (GROUP - 1) * HEAD)], in_send.at[a, h])
    for h in range(MINE):
        wait(kb.at[h, pl.ds(0, SPAN)], z_send.at[0, h])
        wait(vb.at[h, pl.ds(0, SPAN)], z_send.at[1, h])
        wait(halo_s.at[h], h_send.at[h])
    wait(meta.at[pl.ds(0, NY - 1)], m_send.at[0])
    wait(times.at[0, pl.ds(0, NZ - 1)], m_send.at[1])
    wait(times.at[pl.ds(0, NX - 1)], m_send.at[2])
    for h in range(MINE):
        wait(rows_y.at[h, pl.ds(0, NY - 1)], t_send.at[0, h])
        wait(terms.at[h, 0, 0, pl.ds(0, NZ - 1)], t_send.at[1, h])
        wait(terms.at[h, 0, pl.ds(0, NX - 1)], t_send.at[2, h])
        wait(terms.at[h, 0], t_send.at[3, h])


def in_hbm(array):
    return pltpu.with_memory_space_constraint(array, pltpu.HBM)


def local(
    queries, key_states, value_states, out_grad, head_slopes, timesteps, stretch_frames,
    valid_counts, mod_weight,
):
    flat = (PART, WIDTH)
    anywhere = pl.BlockSpec(memory_space=pl.ANY)
    smem = pl.BlockSpec(memory_space=pltpu.SMEM)
    hbm = pl.BlockSpec(memory_space=pltpu.HBM)
    dma = pltpu.SemaphoreType.DMA
    grad = jax.ShapeDtypeStruct(flat, BF16)
    dq, dk, dv, mod = pl.pallas_call(
        main_kernel,
        name="attention_backward",
        out_shape=(pltpu.VMEM(flat, BF16),) * 3 + (pltpu.VMEM((FREQ, WIDTH), F32),),
        in_specs=[smem] * 4 + [hbm] * 5,
        out_specs=(anywhere,) * 3 + (pl.BlockSpec(memory_space=pltpu.VMEM),),
        scratch_shapes=[
            pltpu.VMEM((MINE, NY, TOK, HEAD), BF16),
            pltpu.VMEM((MINE, SLOTS, TOK, HEAD), BF16),
            pltpu.VMEM((MINE, SLOTS, TOK, HEAD), BF16),
            pltpu.VMEM((MINE, NY, TOK, HEAD), BF16),
            pltpu.VMEM((HEAD, SLOTS * TOK), BF16),
            pltpu.VMEM((HEAD, SLOTS * TOK), BF16),
            pltpu.VMEM((FREQ, CHUNK), F32),
            pltpu.VMEM((NY, 8, HEAD), jnp.int32),
            pltpu.VMEM((NX, NZ, NY, 8, HEAD), jnp.int32),
            pltpu.VMEM((NX * NZ * NY, HEAD), F32),
            pltpu.VMEM((MINE, 8, HEAD), F32),
            pltpu.VMEM((NX * NZ * 16, FREQ), F32),
            pltpu.VMEM((FREQ, NX * NZ * 16), BF16),
            pltpu.VMEM((FREQ, NX * NZ * 16), BF16),
            pltpu.VMEM((SLOTS, TOK, HEAD), F32),
            pltpu.VMEM((SPAN + 1, TOK, TOK), F32),
            pltpu.VMEM((SPAN + 1, TOK, TOK), BF16),
            pltpu.VMEM((SPAN + 1, TOK, TOK), BF16),
            pltpu.VMEM((MINE, SLOTS, TOK, HEAD), F32),
            pltpu.VMEM((MINE, SLOTS, TOK, HEAD), F32),
            pltpu.VMEM((MINE, NY, TOK, HEAD), BF16),
            pltpu.VMEM((MINE, NY, TOK, HEAD), BF16),
            pltpu.VMEM((MINE, NY, TOK, HEAD), BF16),
            pltpu.VMEM((MINE, 2, SPAN, TOK, HEAD), BF16),
            pltpu.VMEM((MINE, 2, SPAN, TOK, HEAD), BF16),
            pltpu.VMEM((MINE, 16, HEAD), F32),
            pltpu.VMEM((MINE, NY, 16, HEAD), BF16),
            pltpu.VMEM((MINE, NS, NX, NZ, 16, HEAD), BF16),
            dma((4, MINE)), dma((4, MINE)),
            dma((2, MINE)), dma((2, MINE)),
            dma((MINE,)), dma((MINE,)),
            dma((3,)), dma((3,)), dma((3,)),
            dma((3,)), dma((3,)),
            dma((4, MINE)), dma((4, MINE)),
            dma,
        ],
        compiler_params=pltpu.CompilerParams(
            collective_id=0, has_side_effects=True, vmem_limit_bytes=48 * 2**20
        ),
    )(
        in_hbm(head_slopes), timesteps, stretch_frames,
        valid_counts, in_hbm(mod_weight), in_hbm(queries.reshape(flat)),
        in_hbm(key_states.reshape(flat)), in_hbm(value_states.reshape(flat)),
        in_hbm(out_grad.reshape(flat)),
    )
    whole = (1, 1, PART, WIDTH)
    return dq.reshape(whole), dk.reshape(whole), dv.reshape(whole), mod


def solution(mesh):
    tokens = P("dp", "frame", "spatial", None)
    each = P("dp", "frame")
    return jax.shard_map(
        local,
        mesh=mesh,
        in_specs=(tokens, tokens, tokens, tokens, P(), each, each, each, P()),
        out_specs=(tokens, tokens, tokens, P()),
        check_vma=False,
    )
```

```python
import math

import jax
import jax.numpy as jnp
from jax import lax
from jax.experimental import pallas as pl
from jax.experimental.pallas import tpu as pltpu
from jax.sharding import PartitionSpec as P

MESH = pl.DeviceIdType.MESH
F32 = jnp.float32
BF16 = jnp.bfloat16
HIGHEST = lax.Precision.HIGHEST

NX, NZ, NY, NS = 4, 8, 4, 2
GROUP = NY * NS
SPAN = 3
SLOTS = SPAN + NY
TOK = 256
PART = TOK // NS
HEAD = 128
HEADS = 24
MINE = HEADS // GROUP
CHUNK = MINE * HEAD
WIDTH = HEADS * HEAD
FREQ = 256
SCALE = HEAD ** (-0.5)
LOG2E = math.log2(math.e)
HIDDEN = -1e30
NT = (((1,), (1,)), ((), ()))
TN = (((0,), (0,)), ((), ()))


def dot(a, b, dims=(((1,), (0,)), ((), ()))):
    return lax.dot_general(a, b, dims, preferred_element_type=F32)


def main_kernel(
    slope_ref, step_ref, frame_ref, count_ref, weight_ref,
    q_in, k_in, v_in, g_in,
    dq_out, dk_out, dv_out, mod_out,
    qb, kb, vb, gb, kt, vt, weight, meta, times, rows_t, gate, emb, emb_t, bias,
    x_s, p_s, d_s, dk_acc, dv_acc, dq_s, dk_s, dv_s, halo_s, halo_r, dgate, rows_y, terms,
    in_recv, in_send, z_recv, z_send, h_recv, h_send, o_recv, o_send,
    m_recv, m_send, t_recv, t_send, w_sem,
):
    x = lax.axis_index("dp")
    frame = lax.axis_index("frame")
    s = lax.axis_index("spatial")
    z = frame // NY
    y = frame % NY
    p = y * NS + s

    def group_dev(k):
        other = (p + k) % GROUP
        return (x, z * NY + other // NS, other % NS), other

    def y_dev(k):
        return (x, z * NY + (y + k) % NY, s)

    def z_dev(k):
        return (x, ((z + k) % NZ) * NY + y, s)

    def x_dev(k):
        return ((x + k) % NX, frame, s)

    def loop(low, high, body):
        def step(k, carry):
            body(k)
            return carry

        lax.fori_loop(low, high, step, 0)

    def send(src, dst, send_sem, recv_sem, device):
        pltpu.make_async_remote_copy(
            src_ref=src, dst_ref=dst, send_sem=send_sem, recv_sem=recv_sem,
            device_id=device, device_id_type=MESH,
        ).start()

    def wait(ref, sem):
        pltpu.make_async_copy(ref, ref, sem).wait()

    barrier = pltpu.get_barrier_semaphore()

    def greet(device):
        pl.semaphore_signal(barrier, inc=1, device_id=device, device_id_type=MESH)

    loop(1, GROUP, lambda k: greet(group_dev(k)[0]))
    loop(1, NZ, lambda k: greet(z_dev(k)))
    loop(1, NX, lambda k: greet(x_dev(k)))

    weight_copy = pltpu.make_async_copy(
        weight_ref.at[:, pl.ds(pl.multiple_of(p * CHUNK, HEAD), CHUNK)], weight, w_sem
    )
    weight_copy.start()
    line = lax.broadcasted_iota(jnp.int32, (8, HEAD), 0)
    steps = lax.broadcasted_iota(jnp.int32, (1, HEAD), 1).astype(F32)
    freq = jnp.exp(steps * (-math.log(10000.0) / (FREQ // 2)))
    meta[y] = jnp.where(
        line == 0, count_ref[0, 0], jnp.where(line == 1, frame_ref[0, 0], step_ref[0, 0])
    )
    arrays = ((k_in, kb, SPAN), (v_in, vb, SPAN), (q_in, qb, 0), (g_in, gb, 0))

    def column(owner, h):
        return pl.ds(pl.multiple_of(owner * CHUNK + h * HEAD, HEAD), HEAD)

    def own_part(a, h):
        src, dst, first = arrays[a]
        pltpu.make_async_copy(
            src.at[:, column(p, h)], dst.at[h, first + y, pl.ds(s * PART, PART)], in_recv.at[a, h]
        ).start()

    for a in range(4):
        loop(0, MINE, lambda h, a=a: own_part(a, h))

    pl.semaphore_wait(barrier, GROUP - 1 + NZ - 1 + NX - 1)

    loop(1, NY, lambda k: send(meta.at[y], meta.at[y], m_send.at[0], m_recv.at[0], y_dev(k)))

    def send_part(a, h, k):
        src, dst, first = arrays[a]
        device, owner = group_dev(k)
        send(
            src.at[:, column(owner, h)], dst.at[h, first + y, pl.ds(s * PART, PART)],
            in_send.at[a, h], in_recv.at[a, h], device,
        )

    def send_pair(first, h):
        for a in (first, first + 1):
            loop(1, GROUP, lambda k, a=a: send_part(a, h, k))

    send_pair(0, 0)
    send_pair(2, 0)
    send_pair(0, 1)

    wait(meta.at[pl.ds(0, NY - 1)], m_recv.at[0])
    times[x, z] = meta[...]
    loop(1, NZ, lambda k: send(meta, times.at[x, z], m_send.at[1], m_recv.at[1], z_dev(k)))
    rows_t[...] = jnp.zeros_like(rows_t)
    for i in range(NY):
        rows_t[i : i + 1, :] = meta[i, 2:3, :].astype(F32)
    angles = rows_t[0:8, :] * freq
    own_emb = jnp.concatenate([jnp.cos(angles), jnp.sin(angles)], axis=1)
    weight_copy.wait()
    gates = lax.dot_general(
        own_emb, weight[...], (((1,), (0,)), ((), ())), precision=HIGHEST, preferred_element_type=F32
    )
    for h in range(MINE):
        gate[h] = gates[:, h * HEAD : (h + 1) * HEAD]

    def pass_on(h):
        wait(kb.at[h, pl.ds(SPAN, NY)], in_recv.at[0, h])
        send(
            kb.at[h, pl.ds(NY, SPAN)], kb.at[h, pl.ds(0, SPAN)],
            z_send.at[0, h], z_recv.at[0, h], z_dev(1),
        )
        wait(vb.at[h, pl.ds(SPAN, NY)], in_recv.at[1, h])
        send(
            vb.at[h, pl.ds(NY, SPAN)], vb.at[h, pl.ds(0, SPAN)],
            z_send.at[1, h], z_recv.at[1, h], z_dev(1),
        )

    def arrive(h):
        wait(qb.at[h], in_recv.at[2, h])
        wait(gb.at[h], in_recv.at[3, h])

    pass_on(0)
    send_pair(0, 2)
    wait(times.at[0, pl.ds(0, NZ - 1)], m_recv.at[1])
    loop(1, NX, lambda k: send(times.at[x], times.at[x], m_send.at[2], m_recv.at[2], x_dev(k)))
    arrive(0)
    send_pair(2, 1)
    pass_on(1)
    send_pair(2, 2)

    wait(times.at[pl.ds(0, NX - 1)], m_recv.at[2])

    def take_row(n):
        for i in range(NY):
            rows_t[pl.ds(n * NY + i, 1), :] = times[n // NZ, n % NZ, i, 2:3, :].astype(F32)

    loop(0, NX * NZ, take_row)

    def features(n):
        angle = rows_t[pl.ds(pl.multiple_of(n * 8, 8), 8), :] * freq
        both = jnp.concatenate([jnp.cos(angle), jnp.sin(angle)], axis=1)
        for half in range(2):
            four = both[half * NY : (half + 1) * NY]
            tile = jnp.concatenate([four, four, four, four], axis=0)
            emb[pl.ds(pl.multiple_of(n * 32 + half * 16, 16), 16), :] = tile

    loop(0, NX * NZ // 2, features)
    emb_t[...] = emb[...].T.astype(BF16)

    token = lax.broadcasted_iota(jnp.int32, (TOK, HEAD), 0)
    z_before = (z + NZ - 1) % NZ
    has_before = jnp.minimum(z, 1)
    base = times[x, z, NY - 1, 1:2, :]

    def head(h):
        slope = slope_ref[p * MINE + h] * LOG2E
        for slot in range(SLOTS):
            if slot < SPAN:
                count = times[x, z_before, slot + 1, 0:1, :] * has_before
                place = times[x, z_before, slot + 1, 1:2, :]
            else:
                count = times[x, z, slot - SPAN, 0:1, :]
                place = times[x, z, slot - SPAN, 1:2, :]
            shift = (place - base).astype(F32) * slope
            bias[slot] = jnp.where(token < count, shift, HIDDEN)
        dk_acc[h] = jnp.zeros((SLOTS, TOK, HEAD), F32)
        dv_acc[h] = jnp.zeros((SLOTS, TOK, HEAD), F32)
        wait(kb.at[h, pl.ds(0, SPAN)], z_recv.at[0, h])
        wait(vb.at[h, pl.ds(0, SPAN)], z_recv.at[1, h])
        kt[...] = kb[h].reshape(SLOTS * TOK, HEAD).T
        vt[...] = vb[h].reshape(SLOTS * TOK, HEAD).T
        if h > 0:
            arrive(h)

        def stretch(i):
            q = qb[h, i]
            live = token < times[x, z, i, 0:1, :]
            grad = jnp.where(live, gb[h, i].astype(F32), 0.0)
            go = (gate[h, pl.ds(i, 1), :] * grad).astype(BF16)
            top = jnp.full((1, TOK), HIDDEN, F32)
            for k in range(SPAN + 1):
                one = bias[i + k]
                value = dot(kb[h, i + k], q, NT) * (SCALE * LOG2E) + jnp.concatenate([one, one], axis=1)
                x_s[k] = value
                top = jnp.maximum(top, jnp.max(value, axis=0, keepdims=True))
            total = jnp.zeros((1, TOK), F32)
            for k in range(SPAN + 1):
                value = jnp.exp2(x_s[k] - top)
                x_s[k] = value
                total = total + jnp.sum(value, axis=0, keepdims=True)
            inverse = 1.0 / total
            for k in range(SPAN + 1):
                value = x_s[k] * inverse
                x_s[k] = value
                p_s[k] = value.astype(BF16)
            window = pl.ds(pl.multiple_of(i * TOK, TOK), (SPAN + 1) * TOK)
            out_t = dot(vt[:, window], p_s[...].reshape((SPAN + 1) * TOK, TOK))
            delta = jnp.sum(go.astype(F32).T * out_t, axis=0, keepdims=True)
            dgate[h, pl.ds(y * NY + i, 1), :] = jnp.sum(grad * out_t.T, axis=0, keepdims=True)
            for k in range(SPAN + 1):
                d_s[k] = (x_s[k] * (dot(vb[h, i + k], go, NT) - delta) * SCALE).astype(BF16)
            dq_s[h, i] = dot(kt[:, window], d_s[...].reshape((SPAN + 1) * TOK, TOK)).T.astype(BF16)
            for k in range(SPAN + 1):
                dk_acc[h, i + k] += dot(d_s[k], q)
                dv_acc[h, i + k] += dot(p_s[k], go)

        loop(0, SPAN, stretch)
        halo_s[h, 0] = dk_acc[h, 0:SPAN].astype(BF16)
        halo_s[h, 1] = dv_acc[h, 0:SPAN].astype(BF16)
        send(halo_s.at[h], halo_r.at[h], h_send.at[h], h_recv.at[h], z_dev(NZ - 1))
        stretch(SPAN)

    def give_back(a, staged, out, h):
        def one(k):
            device, owner = group_dev(k)
            send(
                staged.at[h, owner // NS, pl.ds((owner % NS) * PART, PART)], out.at[:, column(p, h)],
                o_send.at[a], o_recv.at[a], device,
            )

        loop(1, GROUP, one)
        out[:, column(p, h)] = staged[h, y, pl.ds(pl.multiple_of(s * PART, PART), PART), :]

    has_after = jnp.minimum(NZ - 1 - z, 1).astype(F32)

    def finish(h):
        wait(halo_r.at[h], h_recv.at[h])
        for n, (acc, staged) in enumerate(((dk_acc, dk_s), (dv_acc, dv_s))):
            staged[h, 0] = acc[h, SPAN].astype(BF16)
            for i in range(1, NY):
                staged[h, i] = (
                    acc[h, SPAN + i] + halo_r[h, n, i - 1].astype(F32) * has_after
                ).astype(BF16)
        give_back(1, dk_s, dk_out, h)
        give_back(2, dv_s, dv_out, h)

    dgate[...] = jnp.zeros_like(dgate)
    def along_y(h):
        rows_y[h, y] = dgate[h].astype(BF16)
        mine = rows_y.at[h, y]
        loop(1, NY, lambda k: send(mine, mine, t_send.at[0, h], t_recv.at[0, h], y_dev(k)))

    def along_z(h):
        wait(rows_y.at[h, pl.ds(0, NY - 1)], t_recv.at[0, h])
        terms[h, s, x, z] = jnp.sum(rows_y[h].astype(F32), axis=0).astype(BF16)
        mine = terms.at[h, s, x, z]
        loop(1, NZ, lambda k: send(mine, mine, t_send.at[1, h], t_recv.at[1, h], z_dev(k)))

    def along_x(h):
        wait(terms.at[h, 0, 0, pl.ds(0, NZ - 1)], t_recv.at[1, h])
        mine = terms.at[h, s, x]
        loop(1, NX, lambda k: send(mine, mine, t_send.at[2, h], t_recv.at[2, h], x_dev(k)))

    def to_core(h):
        wait(terms.at[h, 0, pl.ds(0, NX - 1)], t_recv.at[2, h])
        send(terms.at[h, s], terms.at[h, s], t_send.at[3, h], t_recv.at[3, h], (x, frame, 1 - s))

    row = lax.broadcasted_iota(jnp.int32, (16, HEAD), 0)

    def contract(h):
        wait(terms.at[h, 0], t_recv.at[3, h])
        for other in range(NY):
            keep = jnp.where(row // NY == other, 1.0, 0.0).astype(BF16)
            cores = [(terms[h, core] * keep).reshape(NX * NZ * 16, HEAD) for core in range(NS)]
            both = jnp.concatenate(cores, axis=1)
            part = dot(emb_t[...], both)
            for core in range(NS):
                at = (other * NS + core) * CHUNK + h * HEAD
                mod_out[:, at : at + HEAD] = part[:, core * HEAD : (core + 1) * HEAD]

    head(0)
    along_y(0)
    give_back(0, dq_s, dq_out, 0)
    pass_on(2)
    head(1)
    along_y(1)
    give_back(0, dq_s, dq_out, 1)
    finish(0)
    along_z(0)
    head(2)
    along_y(2)
    along_x(0)
    along_z(1)
    give_back(0, dq_s, dq_out, 2)
    finish(1)
    along_x(1)
    to_core(0)
    along_z(2)
    finish(2)
    along_x(2)
    contract(0)
    to_core(1)
    to_core(2)
    contract(1)
    contract(2)

    outs = (dq_out, dk_out, dv_out)
    arrived = pl.ds(0, (GROUP - 1) * CHUNK)
    for a in range(3):
        wait(outs[a].at[:, arrived], o_recv.at[a])
        wait(outs[a].at[:, arrived], o_send.at[a])
    for a in range(4):
        for h in range(MINE):
            wait(q_in.at[:, pl.ds(0, (GROUP - 1) * HEAD)], in_send.at[a, h])
    for h in range(MINE):
        wait(kb.at[h, pl.ds(0, SPAN)], z_send.at[0, h])
        wait(vb.at[h, pl.ds(0, SPAN)], z_send.at[1, h])
        wait(halo_s.at[h], h_send.at[h])
    wait(meta.at[pl.ds(0, NY - 1)], m_send.at[0])
    wait(times.at[0, pl.ds(0, NZ - 1)], m_send.at[1])
    wait(times.at[pl.ds(0, NX - 1)], m_send.at[2])
    for h in range(MINE):
        wait(rows_y.at[h, pl.ds(0, NY - 1)], t_send.at[0, h])
        wait(terms.at[h, 0, 0, pl.ds(0, NZ - 1)], t_send.at[1, h])
        wait(terms.at[h, 0, pl.ds(0, NX - 1)], t_send.at[2, h])
        wait(terms.at[h, 0], t_send.at[3, h])


def store_kernel(dq, dk, dv, mod, dq_out, dk_out, dv_out, mod_out, sems):
    pairs = ((mod, mod_out), (dq, dq_out), (dk, dk_out), (dv, dv_out))
    copies = [pltpu.make_async_copy(src, dst, sems.at[n]) for n, (src, dst) in enumerate(pairs)]
    for copy in copies:
        copy.start()
    for copy in copies:
        copy.wait()


def in_hbm(array):
    return pltpu.with_memory_space_constraint(array, pltpu.HBM)


def local(
    queries, key_states, value_states, out_grad, head_slopes, timesteps, stretch_frames,
    valid_counts, mod_weight,
):
    flat = (PART, WIDTH)
    anywhere = pl.BlockSpec(memory_space=pl.ANY)
    smem = pl.BlockSpec(memory_space=pltpu.SMEM)
    hbm = pl.BlockSpec(memory_space=pltpu.HBM)
    dma = pltpu.SemaphoreType.DMA
    grad = jax.ShapeDtypeStruct(flat, BF16)
    dq, dk, dv, mod = pl.pallas_call(
        main_kernel,
        name="attention_backward",
        out_shape=(pltpu.VMEM(flat, BF16),) * 3 + (pltpu.VMEM((FREQ, WIDTH), F32),),
        in_specs=[smem] * 4 + [hbm] * 5,
        out_specs=(pl.BlockSpec(memory_space=pltpu.VMEM),) * 4,
        scratch_shapes=[
            pltpu.VMEM((MINE, NY, TOK, HEAD), BF16),
            pltpu.VMEM((MINE, SLOTS, TOK, HEAD), BF16),
            pltpu.VMEM((MINE, SLOTS, TOK, HEAD), BF16),
            pltpu.VMEM((MINE, NY, TOK, HEAD), BF16),
            pltpu.VMEM((HEAD, SLOTS * TOK), BF16),
            pltpu.VMEM((HEAD, SLOTS * TOK), BF16),
            pltpu.VMEM((FREQ, CHUNK), F32),
            pltpu.VMEM((NY, 8, HEAD), jnp.int32),
            pltpu.VMEM((NX, NZ, NY, 8, HEAD), jnp.int32),
            pltpu.VMEM((NX * NZ * NY, HEAD), F32),
            pltpu.VMEM((MINE, 8, HEAD), F32),
            pltpu.VMEM((NX * NZ * 16, FREQ), F32),
            pltpu.VMEM((FREQ, NX * NZ * 16), BF16),
            pltpu.VMEM((SLOTS, TOK, HEAD), F32),
            pltpu.VMEM((SPAN + 1, TOK, TOK), F32),
            pltpu.VMEM((SPAN + 1, TOK, TOK), BF16),
            pltpu.VMEM((SPAN + 1, TOK, TOK), BF16),
            pltpu.VMEM((MINE, SLOTS, TOK, HEAD), F32),
            pltpu.VMEM((MINE, SLOTS, TOK, HEAD), F32),
            pltpu.VMEM((MINE, NY, TOK, HEAD), BF16),
            pltpu.VMEM((MINE, NY, TOK, HEAD), BF16),
            pltpu.VMEM((MINE, NY, TOK, HEAD), BF16),
            pltpu.VMEM((MINE, 2, SPAN, TOK, HEAD), BF16),
            pltpu.VMEM((MINE, 2, SPAN, TOK, HEAD), BF16),
            pltpu.VMEM((MINE, 16, HEAD), F32),
            pltpu.VMEM((MINE, NY, 16, HEAD), BF16),
            pltpu.VMEM((MINE, NS, NX, NZ, 16, HEAD), BF16),
            dma((4, MINE)), dma((4, MINE)),
            dma((2, MINE)), dma((2, MINE)),
            dma((MINE,)), dma((MINE,)),
            dma((3,)), dma((3,)),
            dma((3,)), dma((3,)),
            dma((4, MINE)), dma((4, MINE)),
            dma,
        ],
        compiler_params=pltpu.CompilerParams(
            collective_id=0, has_side_effects=True, vmem_limit_bytes=48 * 2**20
        ),
    )(
        in_hbm(head_slopes), timesteps, stretch_frames,
        valid_counts, in_hbm(mod_weight), in_hbm(queries.reshape(flat)),
        in_hbm(key_states.reshape(flat)), in_hbm(value_states.reshape(flat)),
        in_hbm(out_grad.reshape(flat)),
    )
    dq, dk, dv, mod = pl.pallas_call(
        store_kernel,
        name="store",
        out_shape=(grad, grad, grad, jax.ShapeDtypeStruct((FREQ, WIDTH), F32)),
        in_specs=[pl.BlockSpec(memory_space=pltpu.VMEM)] * 4,
        out_specs=(anywhere,) * 4,
        scratch_shapes=[dma((4,))],
    )(dq, dk, dv, mod)
    whole = (1, 1, PART, WIDTH)
    return dq.reshape(whole), dk.reshape(whole), dv.reshape(whole), mod


def solution(mesh):
    tokens = P("dp", "frame", "spatial", None)
    each = P("dp", "frame")
    return jax.shard_map(
        local,
        mesh=mesh,
        in_specs=(tokens, tokens, tokens, tokens, P(), each, each, each, P()),
        out_specs=(tokens, tokens, tokens, P()),
        check_vma=False,
    )
```

```python
import math

import jax
import jax.numpy as jnp
from jax import lax
from jax.experimental import pallas as pl
from jax.experimental.pallas import tpu as pltpu
from jax.sharding import PartitionSpec as P

MESH = pl.DeviceIdType.MESH
F32 = jnp.float32
BF16 = jnp.bfloat16
HIGHEST = lax.Precision.HIGHEST

NX, NZ, NY, NS = 4, 8, 4, 2
GROUP = NY * NS
SPAN = 3
SLOTS = SPAN + NY
TOK = 256
PART = TOK // NS
HEAD = 128
HEADS = 24
MINE = HEADS // GROUP
CHUNK = MINE * HEAD
WIDTH = HEADS * HEAD
FREQ = 256
SCALE = HEAD ** (-0.5)
LOG2E = math.log2(math.e)
HIDDEN = -1e30
NT = (((1,), (1,)), ((), ()))
TN = (((0,), (0,)), ((), ()))


def dot(a, b, dims=(((1,), (0,)), ((), ()))):
    return lax.dot_general(a, b, dims, preferred_element_type=F32)


def main_kernel(
    slope_ref, step_ref, frame_ref, count_ref, weight_ref,
    q_in, k_in, v_in, g_in,
    dq_out, dk_out, dv_out, mod_out,
    qb, kb, vb, gb, kt, vt, weight, meta, times, rows_t, gate, emb, emb_t, bias,
    x_s, p_s, d_s, dk_acc, dv_acc, dq_s, dk_s, dv_s, halo_s, halo_r, dgate, rows_y, terms,
    in_recv, in_send, z_recv, z_send, h_recv, h_send, o_recv, o_send,
    m_recv, m_send, t_recv, t_send, w_sem,
):
    x = lax.axis_index("dp")
    frame = lax.axis_index("frame")
    s = lax.axis_index("spatial")
    z = frame // NY
    y = frame % NY
    p = y * NS + s

    def group_dev(k):
        other = (p + k) % GROUP
        return (x, z * NY + other // NS, other % NS), other

    def y_dev(k):
        return (x, z * NY + (y + k) % NY, s)

    def z_dev(k):
        return (x, ((z + k) % NZ) * NY + y, s)

    def x_dev(k):
        return ((x + k) % NX, frame, s)

    def loop(low, high, body):
        def step(k, carry):
            body(k)
            return carry

        lax.fori_loop(low, high, step, 0)

    def send(src, dst, send_sem, recv_sem, device):
        pltpu.make_async_remote_copy(
            src_ref=src, dst_ref=dst, send_sem=send_sem, recv_sem=recv_sem,
            device_id=device, device_id_type=MESH,
        ).start()

    def wait(ref, sem):
        pltpu.make_async_copy(ref, ref, sem).wait()

    barrier = pltpu.get_barrier_semaphore()

    def greet(device):
        pl.semaphore_signal(barrier, inc=1, device_id=device, device_id_type=MESH)

    loop(1, GROUP, lambda k: greet(group_dev(k)[0]))
    loop(1, NZ, lambda k: greet(z_dev(k)))
    loop(1, NX, lambda k: greet(x_dev(k)))

    weight_copy = pltpu.make_async_copy(
        weight_ref.at[:, pl.ds(pl.multiple_of(p * CHUNK, HEAD), CHUNK)], weight, w_sem
    )
    weight_copy.start()
    line = lax.broadcasted_iota(jnp.int32, (8, HEAD), 0)
    steps = lax.broadcasted_iota(jnp.int32, (1, HEAD), 1).astype(F32)
    freq = jnp.exp(steps * (-math.log(10000.0) / (FREQ // 2)))
    meta[y] = jnp.where(
        line == 0, count_ref[0, 0], jnp.where(line == 1, frame_ref[0, 0], step_ref[0, 0])
    )
    arrays = ((k_in, kb, SPAN), (v_in, vb, SPAN), (q_in, qb, 0), (g_in, gb, 0))

    def column(owner, h):
        return pl.ds(pl.multiple_of(owner * CHUNK + h * HEAD, HEAD), HEAD)

    def own_part(a, h):
        src, dst, first = arrays[a]
        pltpu.make_async_copy(
            src.at[:, column(p, h)], dst.at[h, first + y, pl.ds(s * PART, PART)], in_recv.at[a, h]
        ).start()

    for a in range(4):
        loop(0, MINE, lambda h, a=a: own_part(a, h))

    pl.semaphore_wait(barrier, GROUP - 1 + NZ - 1 + NX - 1)

    loop(1, NY, lambda k: send(meta.at[y], meta.at[y], m_send.at[0], m_recv.at[0], y_dev(k)))

    def send_part(a, h, k):
        src, dst, first = arrays[a]
        device, owner = group_dev(k)
        send(
            src.at[:, column(owner, h)], dst.at[h, first + y, pl.ds(s * PART, PART)],
            in_send.at[a, h], in_recv.at[a, h], device,
        )

    def send_pair(first, h):
        for a in (first, first + 1):
            loop(1, GROUP, lambda k, a=a: send_part(a, h, k))

    send_pair(0, 0)
    send_pair(2, 0)
    send_pair(0, 1)

    wait(meta.at[pl.ds(0, NY - 1)], m_recv.at[0])
    times[x, z] = meta[...]
    loop(1, NZ, lambda k: send(meta, times.at[x, z], m_send.at[1], m_recv.at[1], z_dev(k)))
    rows_t[...] = jnp.zeros_like(rows_t)
    for i in range(NY):
        rows_t[i : i + 1, :] = meta[i, 2:3, :].astype(F32)
    angles = rows_t[0:8, :] * freq
    own_emb = jnp.concatenate([jnp.cos(angles), jnp.sin(angles)], axis=1)
    weight_copy.wait()
    gates = lax.dot_general(
        own_emb, weight[...], (((1,), (0,)), ((), ())), precision=HIGHEST, preferred_element_type=F32
    )
    for h in range(MINE):
        gate[h] = gates[:, h * HEAD : (h + 1) * HEAD]

    def pass_on(h):
        wait(kb.at[h, pl.ds(SPAN, NY)], in_recv.at[0, h])
        send(
            kb.at[h, pl.ds(NY, SPAN)], kb.at[h, pl.ds(0, SPAN)],
            z_send.at[0, h], z_recv.at[0, h], z_dev(1),
        )
        wait(vb.at[h, pl.ds(SPAN, NY)], in_recv.at[1, h])
        send(
            vb.at[h, pl.ds(NY, SPAN)], vb.at[h, pl.ds(0, SPAN)],
            z_send.at[1, h], z_recv.at[1, h], z_dev(1),
        )

    def arrive(h):
        wait(qb.at[h], in_recv.at[2, h])
        wait(gb.at[h], in_recv.at[3, h])

    pass_on(0)
    send_pair(0, 2)
    wait(times.at[0, pl.ds(0, NZ - 1)], m_recv.at[1])
    loop(1, NX, lambda k: send(times.at[x], times.at[x], m_send.at[2], m_recv.at[2], x_dev(k)))
    arrive(0)
    send_pair(2, 1)
    pass_on(1)
    send_pair(2, 2)

    wait(times.at[pl.ds(0, NX - 1)], m_recv.at[2])

    def take_row(n):
        for i in range(NY):
            rows_t[pl.ds(n * NY + i, 1), :] = times[n // NZ, n % NZ, i, 2:3, :].astype(F32)

    loop(0, NX * NZ, take_row)

    def features(n):
        angle = rows_t[pl.ds(pl.multiple_of(n * 8, 8), 8), :] * freq
        both = jnp.concatenate([jnp.cos(angle), jnp.sin(angle)], axis=1)
        for half in range(2):
            four = both[half * NY : (half + 1) * NY]
            tile = jnp.concatenate([four, four, four, four], axis=0)
            emb[pl.ds(pl.multiple_of(n * 32 + half * 16, 16), 16), :] = tile

    loop(0, NX * NZ // 2, features)
    emb_t[...] = emb[...].T.astype(BF16)

    token = lax.broadcasted_iota(jnp.int32, (TOK, HEAD), 0)
    z_before = (z + NZ - 1) % NZ
    has_before = jnp.minimum(z, 1)
    base = times[x, z, NY - 1, 1:2, :]

    def head(h):
        slope = slope_ref[p * MINE + h] * LOG2E
        for slot in range(SLOTS):
            if slot < SPAN:
                count = times[x, z_before, slot + 1, 0:1, :] * has_before
                place = times[x, z_before, slot + 1, 1:2, :]
            else:
                count = times[x, z, slot - SPAN, 0:1, :]
                place = times[x, z, slot - SPAN, 1:2, :]
            shift = (place - base).astype(F32) * slope
            bias[slot] = jnp.where(token < count, shift, HIDDEN)
        dk_acc[h] = jnp.zeros((SLOTS, TOK, HEAD), F32)
        dv_acc[h] = jnp.zeros((SLOTS, TOK, HEAD), F32)
        wait(kb.at[h, pl.ds(0, SPAN)], z_recv.at[0, h])
        wait(vb.at[h, pl.ds(0, SPAN)], z_recv.at[1, h])
        kt[...] = kb[h].reshape(SLOTS * TOK, HEAD).T
        vt[...] = vb[h].reshape(SLOTS * TOK, HEAD).T
        if h > 0:
            arrive(h)

        def stretch(i):
            q = qb[h, i]
            live = token < times[x, z, i, 0:1, :]
            grad = jnp.where(live, gb[h, i].astype(F32), 0.0)
            go = (gate[h, pl.ds(i, 1), :] * grad).astype(BF16)
            top = jnp.full((1, TOK), HIDDEN, F32)
            for k in range(SPAN + 1):
                one = bias[i + k]
                value = dot(kb[h, i + k], q, NT) * (SCALE * LOG2E) + jnp.concatenate([one, one], axis=1)
                x_s[k] = value
                top = jnp.maximum(top, jnp.max(value, axis=0, keepdims=True))
            total = jnp.zeros((1, TOK), F32)
            for k in range(SPAN + 1):
                value = jnp.exp2(x_s[k] - top)
                x_s[k] = value
                total = total + jnp.sum(value, axis=0, keepdims=True)
            inverse = 1.0 / total
            for k in range(SPAN + 1):
                value = x_s[k] * inverse
                x_s[k] = value
                p_s[k] = value.astype(BF16)
            window = pl.ds(pl.multiple_of(i * TOK, TOK), (SPAN + 1) * TOK)
            out_t = dot(vt[:, window], p_s[...].reshape((SPAN + 1) * TOK, TOK))
            delta = jnp.sum(go.astype(F32).T * out_t, axis=0, keepdims=True)
            dgate[h, pl.ds(y * NY + i, 1), :] = jnp.sum(grad * out_t.T, axis=0, keepdims=True)
            for k in range(SPAN + 1):
                d_s[k] = (x_s[k] * (dot(vb[h, i + k], go, NT) - delta) * SCALE).astype(BF16)
            dq_s[h, i] = dot(kt[:, window], d_s[...].reshape((SPAN + 1) * TOK, TOK)).T.astype(BF16)
            for k in range(SPAN + 1):
                dk_acc[h, i + k] += dot(d_s[k], q)
                dv_acc[h, i + k] += dot(p_s[k], go)

        loop(0, SPAN, stretch)
        halo_s[h, 0] = dk_acc[h, 0:SPAN].astype(BF16)
        halo_s[h, 1] = dv_acc[h, 0:SPAN].astype(BF16)
        send(halo_s.at[h], halo_r.at[h], h_send.at[h], h_recv.at[h], z_dev(NZ - 1))
        stretch(SPAN)

    def give_back(a, staged, out, h):
        def one(k):
            device, owner = group_dev(k)
            send(
                staged.at[h, owner // NS, pl.ds((owner % NS) * PART, PART)], out.at[:, column(p, h)],
                o_send.at[a], o_recv.at[a], device,
            )

        loop(1, GROUP, one)
        out[:, column(p, h)] = staged[h, y, pl.ds(pl.multiple_of(s * PART, PART), PART), :]

    has_after = jnp.minimum(NZ - 1 - z, 1).astype(F32)

    def finish(h):
        wait(halo_r.at[h], h_recv.at[h])
        for n, (acc, staged) in enumerate(((dk_acc, dk_s), (dv_acc, dv_s))):
            staged[h, 0] = acc[h, SPAN].astype(BF16)
            for i in range(1, NY):
                staged[h, i] = (
                    acc[h, SPAN + i] + halo_r[h, n, i - 1].astype(F32) * has_after
                ).astype(BF16)
        give_back(1, dk_s, dk_out, h)
        give_back(2, dv_s, dv_out, h)

    dgate[...] = jnp.zeros_like(dgate)
    def along_y(h):
        rows_y[h, y] = dgate[h].astype(BF16)
        mine = rows_y.at[h, y]
        loop(1, NY, lambda k: send(mine, mine, t_send.at[0, h], t_recv.at[0, h], y_dev(k)))

    def along_z(h):
        wait(rows_y.at[h, pl.ds(0, NY - 1)], t_recv.at[0, h])
        terms[h, s, x, z] = jnp.sum(rows_y[h].astype(F32), axis=0).astype(BF16)
        mine = terms.at[h, s, x, z]
        loop(1, NZ, lambda k: send(mine, mine, t_send.at[1, h], t_recv.at[1, h], z_dev(k)))

    def along_x(h):
        wait(terms.at[h, 0, 0, pl.ds(0, NZ - 1)], t_recv.at[1, h])
        mine = terms.at[h, s, x]
        loop(1, NX, lambda k: send(mine, mine, t_send.at[2, h], t_recv.at[2, h], x_dev(k)))

    def to_core(h):
        wait(terms.at[h, 0, pl.ds(0, NX - 1)], t_recv.at[2, h])
        send(terms.at[h, s], terms.at[h, s], t_send.at[3, h], t_recv.at[3, h], (x, frame, 1 - s))

    row = lax.broadcasted_iota(jnp.int32, (16, HEAD), 0)

    def contract(h):
        wait(terms.at[h, 0], t_recv.at[3, h])
        for other in range(NY):
            keep = jnp.where(row // NY == other, 1.0, 0.0).astype(BF16)
            cores = [(terms[h, core] * keep).reshape(NX * NZ * 16, HEAD) for core in range(NS)]
            both = jnp.concatenate(cores, axis=1)
            part = dot(emb_t[...], both)
            for core in range(NS):
                at = (other * NS + core) * CHUNK + h * HEAD
                mod_out[:, at : at + HEAD] = part[:, core * HEAD : (core + 1) * HEAD]

    head(0)
    along_y(0)
    give_back(0, dq_s, dq_out, 0)
    pass_on(2)
    head(1)
    along_y(1)
    give_back(0, dq_s, dq_out, 1)
    finish(0)
    along_z(0)
    head(2)
    along_y(2)
    along_x(0)
    along_z(1)
    give_back(0, dq_s, dq_out, 2)
    finish(1)
    along_x(1)
    to_core(0)
    along_z(2)
    finish(2)
    along_x(2)
    contract(0)
    to_core(1)
    to_core(2)
    contract(1)
    contract(2)

    outs = (dq_out, dk_out, dv_out)
    arrived = pl.ds(0, (GROUP - 1) * CHUNK)
    for a in range(3):
        wait(outs[a].at[:, arrived], o_recv.at[a])
        wait(outs[a].at[:, arrived], o_send.at[a])
    for a in range(4):
        for h in range(MINE):
            wait(q_in.at[:, pl.ds(0, (GROUP - 1) * HEAD)], in_send.at[a, h])
    for h in range(MINE):
        wait(kb.at[h, pl.ds(0, SPAN)], z_send.at[0, h])
        wait(vb.at[h, pl.ds(0, SPAN)], z_send.at[1, h])
        wait(halo_s.at[h], h_send.at[h])
    wait(meta.at[pl.ds(0, NY - 1)], m_send.at[0])
    wait(times.at[0, pl.ds(0, NZ - 1)], m_send.at[1])
    wait(times.at[pl.ds(0, NX - 1)], m_send.at[2])
    for h in range(MINE):
        wait(rows_y.at[h, pl.ds(0, NY - 1)], t_send.at[0, h])
        wait(terms.at[h, 0, 0, pl.ds(0, NZ - 1)], t_send.at[1, h])
        wait(terms.at[h, 0, pl.ds(0, NX - 1)], t_send.at[2, h])
        wait(terms.at[h, 0], t_send.at[3, h])


def store_kernel(dq, dk, dv, mod, dq_out, dk_out, dv_out, mod_out, sems):
    pairs = ((mod, mod_out), (dq, dq_out), (dk, dk_out), (dv, dv_out))
    copies = [pltpu.make_async_copy(src, dst, sems.at[n]) for n, (src, dst) in enumerate(pairs)]
    for copy in copies:
        copy.start()
    for copy in copies:
        copy.wait()


def in_vmem(array):
    return pltpu.with_memory_space_constraint(array, pltpu.VMEM)


def in_hbm(array):
    return pltpu.with_memory_space_constraint(array, pltpu.HBM)


def local(
    queries, key_states, value_states, out_grad, head_slopes, timesteps, stretch_frames,
    valid_counts, mod_weight,
):
    flat = (PART, WIDTH)
    anywhere = pl.BlockSpec(memory_space=pl.ANY)
    smem = pl.BlockSpec(memory_space=pltpu.SMEM)
    hbm = pl.BlockSpec(memory_space=pltpu.HBM)
    dma = pltpu.SemaphoreType.DMA
    grad = jax.ShapeDtypeStruct(flat, BF16)
    dq, dk, dv, mod = pl.pallas_call(
        main_kernel,
        name="attention_backward",
        out_shape=(pltpu.VMEM(flat, BF16),) * 3 + (pltpu.VMEM((FREQ, WIDTH), F32),),
        in_specs=[smem] * 4 + [hbm] * 5,
        out_specs=(pl.BlockSpec(memory_space=pltpu.VMEM),) * 4,
        scratch_shapes=[
            pltpu.VMEM((MINE, NY, TOK, HEAD), BF16),
            pltpu.VMEM((MINE, SLOTS, TOK, HEAD), BF16),
            pltpu.VMEM((MINE, SLOTS, TOK, HEAD), BF16),
            pltpu.VMEM((MINE, NY, TOK, HEAD), BF16),
            pltpu.VMEM((HEAD, SLOTS * TOK), BF16),
            pltpu.VMEM((HEAD, SLOTS * TOK), BF16),
            pltpu.VMEM((FREQ, CHUNK), F32),
            pltpu.VMEM((NY, 8, HEAD), jnp.int32),
            pltpu.VMEM((NX, NZ, NY, 8, HEAD), jnp.int32),
            pltpu.VMEM((NX * NZ * NY, HEAD), F32),
            pltpu.VMEM((MINE, 8, HEAD), F32),
            pltpu.VMEM((NX * NZ * 16, FREQ), F32),
            pltpu.VMEM((FREQ, NX * NZ * 16), BF16),
            pltpu.VMEM((SLOTS, TOK, HEAD), F32),
            pltpu.VMEM((SPAN + 1, TOK, TOK), F32),
            pltpu.VMEM((SPAN + 1, TOK, TOK), BF16),
            pltpu.VMEM((SPAN + 1, TOK, TOK), BF16),
            pltpu.VMEM((MINE, SLOTS, TOK, HEAD), F32),
            pltpu.VMEM((MINE, SLOTS, TOK, HEAD), F32),
            pltpu.VMEM((MINE, NY, TOK, HEAD), BF16),
            pltpu.VMEM((MINE, NY, TOK, HEAD), BF16),
            pltpu.VMEM((MINE, NY, TOK, HEAD), BF16),
            pltpu.VMEM((MINE, 2, SPAN, TOK, HEAD), BF16),
            pltpu.VMEM((MINE, 2, SPAN, TOK, HEAD), BF16),
            pltpu.VMEM((MINE, 16, HEAD), F32),
            pltpu.VMEM((MINE, NY, 16, HEAD), BF16),
            pltpu.VMEM((MINE, NS, NX, NZ, 16, HEAD), BF16),
            dma((4, MINE)), dma((4, MINE)),
            dma((2, MINE)), dma((2, MINE)),
            dma((MINE,)), dma((MINE,)),
            dma((3,)), dma((3,)),
            dma((3,)), dma((3,)),
            dma((4, MINE)), dma((4, MINE)),
            dma,
        ],
        compiler_params=pltpu.CompilerParams(
            collective_id=0, has_side_effects=True, vmem_limit_bytes=48 * 2**20
        ),
    )(
        in_hbm(head_slopes), timesteps, stretch_frames,
        valid_counts, in_hbm(mod_weight), in_hbm(queries.reshape(flat)),
        in_hbm(key_states.reshape(flat)), in_hbm(value_states.reshape(flat)),
        in_hbm(out_grad.reshape(flat)),
    )
    dq, dk, dv, mod = pl.pallas_call(
        store_kernel,
        name="store",
        out_shape=(pltpu.HBM(flat, BF16),) * 3 + (pltpu.HBM((FREQ, WIDTH), F32),),
        in_specs=[pl.BlockSpec(memory_space=pltpu.VMEM)] * 4,
        out_specs=(anywhere,) * 4,
        scratch_shapes=[dma((4,))],
        compiler_params=pltpu.CompilerParams(vmem_limit_bytes=4 * 2**20),
    )(in_vmem(dq), in_vmem(dk), in_vmem(dv), in_vmem(mod))
    whole = (1, 1, PART, WIDTH)
    return dq.reshape(whole), dk.reshape(whole), dv.reshape(whole), mod


def solution(mesh):
    tokens = P("dp", "frame", "spatial", None)
    each = P("dp", "frame")
    return jax.shard_map(
        local,
        mesh=mesh,
        in_specs=(tokens, tokens, tokens, tokens, P(), each, each, each, P()),
        out_specs=(tokens, tokens, tokens, P()),
        check_vma=False,
    )
```

```python
import math

import jax
import jax.numpy as jnp
from jax import lax
from jax.experimental import pallas as pl
from jax.experimental.pallas import tpu as pltpu
from jax.sharding import PartitionSpec as P

MESH = pl.DeviceIdType.MESH
F32 = jnp.float32
BF16 = jnp.bfloat16
HIGHEST = lax.Precision.HIGHEST

NX, NZ, NY, NS = 4, 8, 4, 2
GROUP = NY * NS
SPAN = 3
SLOTS = SPAN + NY
TOK = 256
PART = TOK // NS
HEAD = 128
HEADS = 24
MINE = HEADS // GROUP
CHUNK = MINE * HEAD
WIDTH = HEADS * HEAD
FREQ = 256
SCALE = HEAD ** (-0.5)
LOG2E = math.log2(math.e)
HIDDEN = -1e30
NT = (((1,), (1,)), ((), ()))
TN = (((0,), (0,)), ((), ()))


def dot(a, b, dims=(((1,), (0,)), ((), ()))):
    return lax.dot_general(a, b, dims, preferred_element_type=F32)


def main_kernel(
    slope_ref, step_ref, frame_ref, count_ref, weight_ref,
    q_in, k_in, v_in, g_in,
    dq_out, dk_out, dv_out, mod_out,
    qb, kb, vb, gb, kt, vt, weight, meta, times, rows_t, gate, emb, emb_t, bias,
    x_s, p_s, d_s, dk_acc, dv_acc, dq_s, dk_s, dv_s, halo_s, halo_r, dgate, rows_y, terms,
    in_recv, in_send, z_recv, z_send, h_recv, h_send, o_recv, o_send,
    m_recv, m_send, t_recv, t_send, w_sem,
):
    x = lax.axis_index("dp")
    frame = lax.axis_index("frame")
    s = lax.axis_index("spatial")
    z = frame // NY
    y = frame % NY
    p = y * NS + s

    def group_dev(k):
        other = (p + k) % GROUP
        return (x, z * NY + other // NS, other % NS), other

    def y_dev(k):
        return (x, z * NY + (y + k) % NY, s)

    def z_dev(k):
        return (x, ((z + k) % NZ) * NY + y, s)

    def x_dev(k):
        return ((x + k) % NX, frame, s)

    def loop(low, high, body):
        def step(k, carry):
            body(k)
            return carry

        lax.fori_loop(low, high, step, 0)

    def send(src, dst, send_sem, recv_sem, device):
        pltpu.make_async_remote_copy(
            src_ref=src, dst_ref=dst, send_sem=send_sem, recv_sem=recv_sem,
            device_id=device, device_id_type=MESH,
        ).start()

    def wait(ref, sem):
        pltpu.make_async_copy(ref, ref, sem).wait()

    barrier = pltpu.get_barrier_semaphore()

    def greet(device):
        pl.semaphore_signal(barrier, inc=1, device_id=device, device_id_type=MESH)

    loop(1, GROUP, lambda k: greet(group_dev(k)[0]))
    loop(1, NZ, lambda k: greet(z_dev(k)))
    loop(1, NX, lambda k: greet(x_dev(k)))

    weight_copy = pltpu.make_async_copy(
        weight_ref.at[:, pl.ds(pl.multiple_of(p * CHUNK, HEAD), CHUNK)], weight, w_sem
    )
    weight_copy.start()
    line = lax.broadcasted_iota(jnp.int32, (8, HEAD), 0)
    steps = lax.broadcasted_iota(jnp.int32, (1, HEAD), 1).astype(F32)
    freq = jnp.exp(steps * (-math.log(10000.0) / (FREQ // 2)))
    meta[y] = jnp.where(
        line == 0, count_ref[0, 0], jnp.where(line == 1, frame_ref[0, 0], step_ref[0, 0])
    )
    arrays = ((k_in, kb, SPAN), (v_in, vb, SPAN), (q_in, qb, 0), (g_in, gb, 0))

    def column(owner, h):
        return pl.ds(pl.multiple_of(owner * CHUNK + h * HEAD, HEAD), HEAD)

    def own_part(a, h):
        src, dst, first = arrays[a]
        pltpu.make_async_copy(
            src.at[:, column(p, h)], dst.at[h, first + y, pl.ds(s * PART, PART)], in_recv.at[a, h]
        ).start()

    for a in range(4):
        loop(0, MINE, lambda h, a=a: own_part(a, h))

    pl.semaphore_wait(barrier, GROUP - 1 + NZ - 1 + NX - 1)

    loop(1, NY, lambda k: send(meta.at[y], meta.at[y], m_send.at[0], m_recv.at[0], y_dev(k)))

    def send_part(a, h, k):
        src, dst, first = arrays[a]
        device, owner = group_dev(k)
        send(
            src.at[:, column(owner, h)], dst.at[h, first + y, pl.ds(s * PART, PART)],
            in_send.at[a, h], in_recv.at[a, h], device,
        )

    def send_pair(first, h):
        for a in (first, first + 1):
            loop(1, GROUP, lambda k, a=a: send_part(a, h, k))

    send_pair(0, 0)
    send_pair(0, 1)
    send_pair(2, 0)

    wait(meta.at[pl.ds(0, NY - 1)], m_recv.at[0])
    times[x, z] = meta[...]
    loop(1, NZ, lambda k: send(meta, times.at[x, z], m_send.at[1], m_recv.at[1], z_dev(k)))
    rows_t[...] = jnp.zeros_like(rows_t)
    for i in range(NY):
        rows_t[i : i + 1, :] = meta[i, 2:3, :].astype(F32)
    angles = rows_t[0:8, :] * freq
    own_emb = jnp.concatenate([jnp.cos(angles), jnp.sin(angles)], axis=1)
    weight_copy.wait()
    gates = lax.dot_general(
        own_emb, weight[...], (((1,), (0,)), ((), ())), precision=HIGHEST, preferred_element_type=F32
    )
    for h in range(MINE):
        gate[h] = gates[:, h * HEAD : (h + 1) * HEAD]

    def pass_on(h):
        wait(kb.at[h, pl.ds(SPAN, NY)], in_recv.at[0, h])
        send(
            kb.at[h, pl.ds(NY, SPAN)], kb.at[h, pl.ds(0, SPAN)],
            z_send.at[0, h], z_recv.at[0, h], z_dev(1),
        )
        wait(vb.at[h, pl.ds(SPAN, NY)], in_recv.at[1, h])
        send(
            vb.at[h, pl.ds(NY, SPAN)], vb.at[h, pl.ds(0, SPAN)],
            z_send.at[1, h], z_recv.at[1, h], z_dev(1),
        )

    def arrive(h):
        wait(qb.at[h], in_recv.at[2, h])
        wait(gb.at[h], in_recv.at[3, h])

    pass_on(0)
    send_pair(0, 2)
    wait(times.at[0, pl.ds(0, NZ - 1)], m_recv.at[1])
    loop(1, NX, lambda k: send(times.at[x], times.at[x], m_send.at[2], m_recv.at[2], x_dev(k)))
    pass_on(1)
    send_pair(2, 1)
    arrive(0)
    send_pair(2, 2)

    wait(times.at[pl.ds(0, NX - 1)], m_recv.at[2])

    def take_row(n):
        for i in range(NY):
            rows_t[pl.ds(n * NY + i, 1), :] = times[n // NZ, n % NZ, i, 2:3, :].astype(F32)

    loop(0, NX * NZ, take_row)

    def features(n):
        angle = rows_t[pl.ds(pl.multiple_of(n * 8, 8), 8), :] * freq
        both = jnp.concatenate([jnp.cos(angle), jnp.sin(angle)], axis=1)
        for half in range(2):
            four = both[half * NY : (half + 1) * NY]
            tile = jnp.concatenate([four, four, four, four], axis=0)
            emb[pl.ds(pl.multiple_of(n * 32 + half * 16, 16), 16), :] = tile

    loop(0, NX * NZ // 2, features)
    emb_t[...] = emb[...].T.astype(BF16)

    token = lax.broadcasted_iota(jnp.int32, (TOK, HEAD), 0)
    z_before = (z + NZ - 1) % NZ
    has_before = jnp.minimum(z, 1)
    base = times[x, z, NY - 1, 1:2, :]

    def head(h):
        slope = slope_ref[p * MINE + h] * LOG2E
        for slot in range(SLOTS):
            if slot < SPAN:
                count = times[x, z_before, slot + 1, 0:1, :] * has_before
                place = times[x, z_before, slot + 1, 1:2, :]
            else:
                count = times[x, z, slot - SPAN, 0:1, :]
                place = times[x, z, slot - SPAN, 1:2, :]
            shift = (place - base).astype(F32) * slope
            bias[slot] = jnp.where(token < count, shift, HIDDEN)
        dk_acc[h] = jnp.zeros((SLOTS, TOK, HEAD), F32)
        dv_acc[h] = jnp.zeros((SLOTS, TOK, HEAD), F32)
        wait(kb.at[h, pl.ds(0, SPAN)], z_recv.at[0, h])
        wait(vb.at[h, pl.ds(0, SPAN)], z_recv.at[1, h])
        kt[...] = kb[h].reshape(SLOTS * TOK, HEAD).T
        vt[...] = vb[h].reshape(SLOTS * TOK, HEAD).T
        if h > 0:
            arrive(h)

        def stretch(i):
            q = qb[h, i]
            live = token < times[x, z, i, 0:1, :]
            grad = jnp.where(live, gb[h, i].astype(F32), 0.0)
            go = (gate[h, pl.ds(i, 1), :] * grad).astype(BF16)
            top = jnp.full((1, TOK), HIDDEN, F32)
            for k in range(SPAN + 1):
                one = bias[i + k]
                value = dot(kb[h, i + k], q, NT) * (SCALE * LOG2E) + jnp.concatenate([one, one], axis=1)
                x_s[k] = value
                top = jnp.maximum(top, jnp.max(value, axis=0, keepdims=True))
            total = jnp.zeros((1, TOK), F32)
            for k in range(SPAN + 1):
                value = jnp.exp2(x_s[k] - top)
                x_s[k] = value
                total = total + jnp.sum(value, axis=0, keepdims=True)
            inverse = 1.0 / total
            for k in range(SPAN + 1):
                value = x_s[k] * inverse
                x_s[k] = value
                p_s[k] = value.astype(BF16)
            window = pl.ds(pl.multiple_of(i * TOK, TOK), (SPAN + 1) * TOK)
            out_t = dot(vt[:, window], p_s[...].reshape((SPAN + 1) * TOK, TOK))
            delta = jnp.sum(go.astype(F32).T * out_t, axis=0, keepdims=True)
            dgate[h, pl.ds(y * NY + i, 1), :] = jnp.sum(grad * out_t.T, axis=0, keepdims=True)
            for k in range(SPAN + 1):
                d_s[k] = (x_s[k] * (dot(vb[h, i + k], go, NT) - delta) * SCALE).astype(BF16)
            dq_s[h, i] = dot(kt[:, window], d_s[...].reshape((SPAN + 1) * TOK, TOK)).T.astype(BF16)
            for k in range(SPAN + 1):
                dk_acc[h, i + k] += dot(d_s[k], q)
                dv_acc[h, i + k] += dot(p_s[k], go)

        loop(0, SPAN, stretch)
        halo_s[h, 0] = dk_acc[h, 0:SPAN].astype(BF16)
        halo_s[h, 1] = dv_acc[h, 0:SPAN].astype(BF16)
        send(halo_s.at[h], halo_r.at[h], h_send.at[h], h_recv.at[h], z_dev(NZ - 1))
        stretch(SPAN)

    def give_back(a, staged, out, h):
        def one(k):
            device, owner = group_dev(k)
            send(
                staged.at[h, owner // NS, pl.ds((owner % NS) * PART, PART)], out.at[:, column(p, h)],
                o_send.at[a], o_recv.at[a], device,
            )

        loop(1, GROUP, one)
        out[:, column(p, h)] = staged[h, y, pl.ds(pl.multiple_of(s * PART, PART), PART), :]

    has_after = jnp.minimum(NZ - 1 - z, 1).astype(F32)

    def finish(h):
        wait(halo_r.at[h], h_recv.at[h])
        for n, (acc, staged) in enumerate(((dk_acc, dk_s), (dv_acc, dv_s))):
            staged[h, 0] = acc[h, SPAN].astype(BF16)
            for i in range(1, NY):
                staged[h, i] = (
                    acc[h, SPAN + i] + halo_r[h, n, i - 1].astype(F32) * has_after
                ).astype(BF16)
        give_back(1, dk_s, dk_out, h)
        give_back(2, dv_s, dv_out, h)

    dgate[...] = jnp.zeros_like(dgate)
    def along_y(h):
        rows_y[h, y] = dgate[h].astype(BF16)
        mine = rows_y.at[h, y]
        loop(1, NY, lambda k: send(mine, mine, t_send.at[0, h], t_recv.at[0, h], y_dev(k)))

    def along_z(h):
        wait(rows_y.at[h, pl.ds(0, NY - 1)], t_recv.at[0, h])
        terms[h, s, x, z] = jnp.sum(rows_y[h].astype(F32), axis=0).astype(BF16)
        mine = terms.at[h, s, x, z]
        loop(1, NZ, lambda k: send(mine, mine, t_send.at[1, h], t_recv.at[1, h], z_dev(k)))

    def along_x(h):
        wait(terms.at[h, 0, 0, pl.ds(0, NZ - 1)], t_recv.at[1, h])
        mine = terms.at[h, s, x]
        loop(1, NX, lambda k: send(mine, mine, t_send.at[2, h], t_recv.at[2, h], x_dev(k)))

    def to_core(h):
        wait(terms.at[h, 0, pl.ds(0, NX - 1)], t_recv.at[2, h])
        send(terms.at[h, s], terms.at[h, s], t_send.at[3, h], t_recv.at[3, h], (x, frame, 1 - s))

    row = lax.broadcasted_iota(jnp.int32, (16, HEAD), 0)

    def contract(h):
        wait(terms.at[h, 0], t_recv.at[3, h])
        for other in range(NY):
            keep = jnp.where(row // NY == other, 1.0, 0.0).astype(BF16)
            cores = [(terms[h, core] * keep).reshape(NX * NZ * 16, HEAD) for core in range(NS)]
            both = jnp.concatenate(cores, axis=1)
            part = dot(emb_t[...], both)
            for core in range(NS):
                at = (other * NS + core) * CHUNK + h * HEAD
                mod_out[:, at : at + HEAD] = part[:, core * HEAD : (core + 1) * HEAD]

    head(0)
    along_y(0)
    give_back(0, dq_s, dq_out, 0)
    pass_on(2)
    head(1)
    along_y(1)
    give_back(0, dq_s, dq_out, 1)
    finish(0)
    along_z(0)
    head(2)
    along_y(2)
    along_x(0)
    along_z(1)
    give_back(0, dq_s, dq_out, 2)
    finish(1)
    along_x(1)
    to_core(0)
    along_z(2)
    finish(2)
    along_x(2)
    contract(0)
    to_core(1)
    to_core(2)
    contract(1)
    contract(2)

    outs = (dq_out, dk_out, dv_out)
    arrived = pl.ds(0, (GROUP - 1) * CHUNK)
    for a in range(3):
        wait(outs[a].at[:, arrived], o_recv.at[a])
        wait(outs[a].at[:, arrived], o_send.at[a])
    for a in range(4):
        for h in range(MINE):
            wait(q_in.at[:, pl.ds(0, (GROUP - 1) * HEAD)], in_send.at[a, h])
    for h in range(MINE):
        wait(kb.at[h, pl.ds(0, SPAN)], z_send.at[0, h])
        wait(vb.at[h, pl.ds(0, SPAN)], z_send.at[1, h])
        wait(halo_s.at[h], h_send.at[h])
    wait(meta.at[pl.ds(0, NY - 1)], m_send.at[0])
    wait(times.at[0, pl.ds(0, NZ - 1)], m_send.at[1])
    wait(times.at[pl.ds(0, NX - 1)], m_send.at[2])
    for h in range(MINE):
        wait(rows_y.at[h, pl.ds(0, NY - 1)], t_send.at[0, h])
        wait(terms.at[h, 0, 0, pl.ds(0, NZ - 1)], t_send.at[1, h])
        wait(terms.at[h, 0, pl.ds(0, NX - 1)], t_send.at[2, h])
        wait(terms.at[h, 0], t_send.at[3, h])


def store_kernel(dq, dk, dv, mod, dq_out, dk_out, dv_out, mod_out, sems):
    pairs = ((mod, mod_out), (dq, dq_out), (dk, dk_out), (dv, dv_out))
    copies = [pltpu.make_async_copy(src, dst, sems.at[n]) for n, (src, dst) in enumerate(pairs)]
    for copy in copies:
        copy.start()
    for copy in copies:
        copy.wait()


def in_vmem(array):
    return pltpu.with_memory_space_constraint(array, pltpu.VMEM)


def in_hbm(array):
    return pltpu.with_memory_space_constraint(array, pltpu.HBM)


def local(
    queries, key_states, value_states, out_grad, head_slopes, timesteps, stretch_frames,
    valid_counts, mod_weight,
):
    flat = (PART, WIDTH)
    anywhere = pl.BlockSpec(memory_space=pl.ANY)
    smem = pl.BlockSpec(memory_space=pltpu.SMEM)
    hbm = pl.BlockSpec(memory_space=pltpu.HBM)
    dma = pltpu.SemaphoreType.DMA
    grad = jax.ShapeDtypeStruct(flat, BF16)
    dq, dk, dv, mod = pl.pallas_call(
        main_kernel,
        name="attention_backward",
        out_shape=(pltpu.VMEM(flat, BF16),) * 3 + (pltpu.VMEM((FREQ, WIDTH), F32),),
        in_specs=[smem] * 4 + [hbm] * 5,
        out_specs=(pl.BlockSpec(memory_space=pltpu.VMEM),) * 4,
        scratch_shapes=[
            pltpu.VMEM((MINE, NY, TOK, HEAD), BF16),
            pltpu.VMEM((MINE, SLOTS, TOK, HEAD), BF16),
            pltpu.VMEM((MINE, SLOTS, TOK, HEAD), BF16),
            pltpu.VMEM((MINE, NY, TOK, HEAD), BF16),
            pltpu.VMEM((HEAD, SLOTS * TOK), BF16),
            pltpu.VMEM((HEAD, SLOTS * TOK), BF16),
            pltpu.VMEM((FREQ, CHUNK), F32),
            pltpu.VMEM((NY, 8, HEAD), jnp.int32),
            pltpu.VMEM((NX, NZ, NY, 8, HEAD), jnp.int32),
            pltpu.VMEM((NX * NZ * NY, HEAD), F32),
            pltpu.VMEM((MINE, 8, HEAD), F32),
            pltpu.VMEM((NX * NZ * 16, FREQ), F32),
            pltpu.VMEM((FREQ, NX * NZ * 16), BF16),
            pltpu.VMEM((SLOTS, TOK, HEAD), F32),
            pltpu.VMEM((SPAN + 1, TOK, TOK), F32),
            pltpu.VMEM((SPAN + 1, TOK, TOK), BF16),
            pltpu.VMEM((SPAN + 1, TOK, TOK), BF16),
            pltpu.VMEM((MINE, SLOTS, TOK, HEAD), F32),
            pltpu.VMEM((MINE, SLOTS, TOK, HEAD), F32),
            pltpu.VMEM((MINE, NY, TOK, HEAD), BF16),
            pltpu.VMEM((MINE, NY, TOK, HEAD), BF16),
            pltpu.VMEM((MINE, NY, TOK, HEAD), BF16),
            pltpu.VMEM((MINE, 2, SPAN, TOK, HEAD), BF16),
            pltpu.VMEM((MINE, 2, SPAN, TOK, HEAD), BF16),
            pltpu.VMEM((MINE, 16, HEAD), F32),
            pltpu.VMEM((MINE, NY, 16, HEAD), BF16),
            pltpu.VMEM((MINE, NS, NX, NZ, 16, HEAD), BF16),
            dma((4, MINE)), dma((4, MINE)),
            dma((2, MINE)), dma((2, MINE)),
            dma((MINE,)), dma((MINE,)),
            dma((3,)), dma((3,)),
            dma((3,)), dma((3,)),
            dma((4, MINE)), dma((4, MINE)),
            dma,
        ],
        compiler_params=pltpu.CompilerParams(
            collective_id=0, has_side_effects=True, vmem_limit_bytes=48 * 2**20
        ),
    )(
        in_hbm(head_slopes), timesteps, stretch_frames,
        valid_counts, in_hbm(mod_weight), in_hbm(queries.reshape(flat)),
        in_hbm(key_states.reshape(flat)), in_hbm(value_states.reshape(flat)),
        in_hbm(out_grad.reshape(flat)),
    )
    dq, dk, dv, mod = pl.pallas_call(
        store_kernel,
        name="store",
        out_shape=(pltpu.HBM(flat, BF16),) * 3 + (pltpu.HBM((FREQ, WIDTH), F32),),
        in_specs=[pl.BlockSpec(memory_space=pltpu.VMEM)] * 4,
        out_specs=(anywhere,) * 4,
        scratch_shapes=[dma((4,))],
        compiler_params=pltpu.CompilerParams(vmem_limit_bytes=4 * 2**20),
    )(in_vmem(dq), in_vmem(dk), in_vmem(dv), in_vmem(mod))
    whole = (1, 1, PART, WIDTH)
    return dq.reshape(whole), dk.reshape(whole), dv.reshape(whole), mod


def solution(mesh):
    tokens = P("dp", "frame", "spatial", None)
    each = P("dp", "frame")
    return jax.shard_map(
        local,
        mesh=mesh,
        in_specs=(tokens, tokens, tokens, tokens, P(), each, each, each, P()),
        out_specs=(tokens, tokens, tokens, P()),
        check_vma=False,
    )
```

```python
import math

import jax
import jax.numpy as jnp
from jax import lax
from jax.experimental import pallas as pl
from jax.experimental.pallas import tpu as pltpu
from jax.sharding import PartitionSpec as P

MESH = pl.DeviceIdType.MESH
F32 = jnp.float32
BF16 = jnp.bfloat16
HIGHEST = lax.Precision.HIGHEST

NX, NZ, NY, NS = 4, 8, 4, 2
GROUP = NY * NS
SPAN = 3
SLOTS = SPAN + NY
TOK = 256
PART = TOK // NS
HEAD = 128
HEADS = 24
MINE = HEADS // GROUP
CHUNK = MINE * HEAD
WIDTH = HEADS * HEAD
FREQ = 256
SCALE = HEAD ** (-0.5)
LOG2E = math.log2(math.e)
HIDDEN = -1e30
NT = (((1,), (1,)), ((), ()))
TN = (((0,), (0,)), ((), ()))


def dot(a, b, dims=(((1,), (0,)), ((), ()))):
    return lax.dot_general(a, b, dims, preferred_element_type=F32)


def main_kernel(
    slope_ref, step_ref, frame_ref, count_ref, weight_ref,
    q_in, k_in, v_in, g_in,
    dq_out, dk_out, dv_out, mod_out,
    qb, kb, vb, gb, kt, vt, weight, meta, times, rows_t, gate, emb, emb_t, bias,
    x_s, p_s, d_s, dk_acc, dv_acc, dq_s, dk_s, dv_s, halo_s, halo_r, dgate, rows_y, terms,
    in_recv, in_send, z_recv, z_send, h_recv, h_send, o_recv, o_send,
    m_recv, m_send, t_recv, t_send, w_sem,
):
    x = lax.axis_index("dp")
    frame = lax.axis_index("frame")
    s = lax.axis_index("spatial")
    z = frame // NY
    y = frame % NY
    p = y * NS + s

    def group_dev(k):
        other = (p + k) % GROUP
        return (x, z * NY + other // NS, other % NS), other

    def y_dev(k):
        return (x, z * NY + (y + k) % NY, s)

    def z_dev(k):
        return (x, ((z + k) % NZ) * NY + y, s)

    def x_dev(k):
        return ((x + k) % NX, frame, s)

    def loop(low, high, body):
        def step(k, carry):
            body(k)
            return carry

        lax.fori_loop(low, high, step, 0)

    def send(src, dst, send_sem, recv_sem, device):
        pltpu.make_async_remote_copy(
            src_ref=src, dst_ref=dst, send_sem=send_sem, recv_sem=recv_sem,
            device_id=device, device_id_type=MESH,
        ).start()

    def wait(ref, sem):
        pltpu.make_async_copy(ref, ref, sem).wait()

    barrier = pltpu.get_barrier_semaphore()

    def greet(device):
        pl.semaphore_signal(barrier, inc=1, device_id=device, device_id_type=MESH)

    loop(1, GROUP, lambda k: greet(group_dev(k)[0]))
    loop(1, NZ, lambda k: greet(z_dev(k)))
    loop(1, NX, lambda k: greet(x_dev(k)))

    weight_copy = pltpu.make_async_copy(
        weight_ref.at[:, pl.ds(pl.multiple_of(p * CHUNK, HEAD), CHUNK)], weight, w_sem
    )
    weight_copy.start()
    line = lax.broadcasted_iota(jnp.int32, (8, HEAD), 0)
    steps = lax.broadcasted_iota(jnp.int32, (1, HEAD), 1).astype(F32)
    freq = jnp.exp(steps * (-math.log(10000.0) / (FREQ // 2)))
    meta[y] = jnp.where(
        line == 0, count_ref[0, 0], jnp.where(line == 1, frame_ref[0, 0], step_ref[0, 0])
    )
    arrays = ((k_in, kb, SPAN), (v_in, vb, SPAN), (q_in, qb, 0), (g_in, gb, 0))

    def column(owner, h):
        return pl.ds(pl.multiple_of(owner * CHUNK + h * HEAD, HEAD), HEAD)

    def own_part(a, h):
        src, dst, first = arrays[a]
        pltpu.make_async_copy(
            src.at[:, column(p, h)], dst.at[h, first + y, pl.ds(s * PART, PART)], in_recv.at[a, h]
        ).start()

    for a in range(4):
        loop(0, MINE, lambda h, a=a: own_part(a, h))

    pl.semaphore_wait(barrier, GROUP - 1 + NZ - 1 + NX - 1)

    loop(1, NY, lambda k: send(meta.at[y], meta.at[y], m_send.at[0], m_recv.at[0], y_dev(k)))

    def send_part(a, h, k):
        src, dst, first = arrays[a]
        device, owner = group_dev(k)
        send(
            src.at[:, column(owner, h)], dst.at[h, first + y, pl.ds(s * PART, PART)],
            in_send.at[a, h], in_recv.at[a, h], device,
        )

    def send_pair(first, h):
        for a in (first, first + 1):
            loop(1, GROUP, lambda k, a=a: send_part(a, h, k))

    send_pair(0, 0)
    send_pair(2, 0)
    send_pair(0, 1)

    wait(meta.at[pl.ds(0, NY - 1)], m_recv.at[0])
    times[x, z] = meta[...]
    loop(1, NZ, lambda k: send(meta, times.at[x, z], m_send.at[1], m_recv.at[1], z_dev(k)))
    rows_t[...] = jnp.zeros_like(rows_t)
    for i in range(NY):
        rows_t[i : i + 1, :] = meta[i, 2:3, :].astype(F32)
    angles = rows_t[0:8, :] * freq
    own_emb = jnp.concatenate([jnp.cos(angles), jnp.sin(angles)], axis=1)
    weight_copy.wait()
    gates = lax.dot_general(
        own_emb, weight[...], (((1,), (0,)), ((), ())), precision=HIGHEST, preferred_element_type=F32
    )
    for h in range(MINE):
        gate[h] = gates[:, h * HEAD : (h + 1) * HEAD]

    def pass_on(h):
        wait(kb.at[h, pl.ds(SPAN, NY)], in_recv.at[0, h])
        send(
            kb.at[h, pl.ds(NY, SPAN)], kb.at[h, pl.ds(0, SPAN)],
            z_send.at[0, h], z_recv.at[0, h], z_dev(1),
        )
        wait(vb.at[h, pl.ds(SPAN, NY)], in_recv.at[1, h])
        send(
            vb.at[h, pl.ds(NY, SPAN)], vb.at[h, pl.ds(0, SPAN)],
            z_send.at[1, h], z_recv.at[1, h], z_dev(1),
        )

    def arrive(h):
        wait(qb.at[h], in_recv.at[2, h])
        wait(gb.at[h], in_recv.at[3, h])

    pass_on(0)
    send_pair(0, 2)
    wait(times.at[0, pl.ds(0, NZ - 1)], m_recv.at[1])
    loop(1, NX, lambda k: send(times.at[x], times.at[x], m_send.at[2], m_recv.at[2], x_dev(k)))
    arrive(0)
    send_pair(2, 1)
    pass_on(1)
    send_pair(2, 2)

    wait(times.at[pl.ds(0, NX - 1)], m_recv.at[2])

    def take_row(n):
        for i in range(NY):
            rows_t[pl.ds(n * NY + i, 1), :] = times[n // NZ, n % NZ, i, 2:3, :].astype(F32)

    loop(0, NX * NZ, take_row)

    def features(n):
        angle = rows_t[pl.ds(pl.multiple_of(n * 8, 8), 8), :] * freq
        both = jnp.concatenate([jnp.cos(angle), jnp.sin(angle)], axis=1)
        for half in range(2):
            four = both[half * NY : (half + 1) * NY]
            tile = jnp.concatenate([four, four, four, four], axis=0)
            emb[pl.ds(pl.multiple_of(n * 32 + half * 16, 16), 16), :] = tile

    loop(0, NX * NZ // 2, features)
    emb_t[...] = emb[...].T.astype(BF16)

    token = lax.broadcasted_iota(jnp.int32, (TOK, HEAD), 0)
    z_before = (z + NZ - 1) % NZ
    has_before = jnp.minimum(z, 1)
    base = times[x, z, NY - 1, 1:2, :]

    def head(h):
        slope = slope_ref[p * MINE + h] * LOG2E
        for slot in range(SLOTS):
            if slot < SPAN:
                count = times[x, z_before, slot + 1, 0:1, :] * has_before
                place = times[x, z_before, slot + 1, 1:2, :]
            else:
                count = times[x, z, slot - SPAN, 0:1, :]
                place = times[x, z, slot - SPAN, 1:2, :]
            shift = (place - base).astype(F32) * slope
            bias[slot] = jnp.where(token < count, shift, HIDDEN)
        dk_acc[h] = jnp.zeros((SLOTS, TOK, HEAD), F32)
        dv_acc[h] = jnp.zeros((SLOTS, TOK, HEAD), F32)
        wait(kb.at[h, pl.ds(0, SPAN)], z_recv.at[0, h])
        wait(vb.at[h, pl.ds(0, SPAN)], z_recv.at[1, h])
        kt[...] = kb[h].reshape(SLOTS * TOK, HEAD).T
        vt[...] = vb[h].reshape(SLOTS * TOK, HEAD).T
        if h > 0:
            arrive(h)

        def stretch(i):
            q = qb[h, i]
            live = token < times[x, z, i, 0:1, :]
            grad = jnp.where(live, gb[h, i].astype(F32), 0.0)
            go = (gate[h, pl.ds(i, 1), :] * grad).astype(BF16)
            top = jnp.full((1, TOK), HIDDEN, F32)
            for k in range(SPAN + 1):
                one = bias[i + k]
                value = dot(kb[h, i + k], q, NT) * (SCALE * LOG2E) + jnp.concatenate([one, one], axis=1)
                x_s[k] = value
                top = jnp.maximum(top, jnp.max(value, axis=0, keepdims=True))
            total = jnp.zeros((1, TOK), F32)
            for k in range(SPAN + 1):
                value = jnp.exp2(x_s[k] - top)
                x_s[k] = value
                total = total + jnp.sum(value, axis=0, keepdims=True)
            inverse = 1.0 / total
            for k in range(SPAN + 1):
                value = x_s[k] * inverse
                x_s[k] = value
                p_s[k] = value.astype(BF16)
            window = pl.ds(pl.multiple_of(i * TOK, TOK), (SPAN + 1) * TOK)
            out_t = dot(vt[:, window], p_s[...].reshape((SPAN + 1) * TOK, TOK))
            delta = jnp.sum(go.astype(F32).T * out_t, axis=0, keepdims=True)
            dgate[h, pl.ds(y * NY + i, 1), :] = jnp.sum(grad * out_t.T, axis=0, keepdims=True)
            for k in range(SPAN + 1):
                d_s[k] = (x_s[k] * (dot(vb[h, i + k], go, NT) - delta) * SCALE).astype(BF16)
            dq_s[h, i] = dot(kt[:, window], d_s[...].reshape((SPAN + 1) * TOK, TOK)).T.astype(BF16)
            for k in range(SPAN + 1):
                dk_acc[h, i + k] += dot(d_s[k], q)
                dv_acc[h, i + k] += dot(p_s[k], go)

        loop(0, SPAN, stretch)
        halo_s[h, 0] = dk_acc[h, 0:SPAN].astype(BF16)
        halo_s[h, 1] = dv_acc[h, 0:SPAN].astype(BF16)
        for n in range(2):
            send(
                halo_s.at[h, n], halo_r.at[h, n], h_send.at[n, h], h_recv.at[n, h], z_dev(NZ - 1)
            )
        stretch(SPAN)

    def give_back(a, staged, out, h):
        def one(k):
            device, owner = group_dev(k)
            send(
                staged.at[h, owner // NS, pl.ds((owner % NS) * PART, PART)], out.at[:, column(p, h)],
                o_send.at[a], o_recv.at[a], device,
            )

        loop(1, GROUP, one)
        out[:, column(p, h)] = staged[h, y, pl.ds(pl.multiple_of(s * PART, PART), PART), :]

    has_after = jnp.minimum(NZ - 1 - z, 1).astype(F32)

    def finish(h):
        for n, (acc, staged, out) in enumerate(((dk_acc, dk_s, dk_out), (dv_acc, dv_s, dv_out))):
            wait(halo_r.at[h, n], h_recv.at[n, h])
            staged[h, 0] = acc[h, SPAN].astype(BF16)
            for i in range(1, NY):
                staged[h, i] = (
                    acc[h, SPAN + i] + halo_r[h, n, i - 1].astype(F32) * has_after
                ).astype(BF16)
            give_back(1 + n, staged, out, h)

    dgate[...] = jnp.zeros_like(dgate)
    def along_y(h):
        rows_y[h, y] = dgate[h].astype(BF16)
        mine = rows_y.at[h, y]
        loop(1, NY, lambda k: send(mine, mine, t_send.at[0, h], t_recv.at[0, h], y_dev(k)))

    def along_z(h):
        wait(rows_y.at[h, pl.ds(0, NY - 1)], t_recv.at[0, h])
        terms[h, s, x, z] = jnp.sum(rows_y[h].astype(F32), axis=0).astype(BF16)
        mine = terms.at[h, s, x, z]
        loop(1, NZ, lambda k: send(mine, mine, t_send.at[1, h], t_recv.at[1, h], z_dev(k)))

    def along_x(h):
        wait(terms.at[h, 0, 0, pl.ds(0, NZ - 1)], t_recv.at[1, h])
        mine = terms.at[h, s, x]
        loop(1, NX, lambda k: send(mine, mine, t_send.at[2, h], t_recv.at[2, h], x_dev(k)))

    def to_core(h):
        wait(terms.at[h, 0, pl.ds(0, NX - 1)], t_recv.at[2, h])
        send(terms.at[h, s], terms.at[h, s], t_send.at[3, h], t_recv.at[3, h], (x, frame, 1 - s))

    row = lax.broadcasted_iota(jnp.int32, (16, HEAD), 0)

    def contract(h):
        wait(terms.at[h, 0], t_recv.at[3, h])
        for other in range(NY):
            keep = jnp.where(row // NY == other, 1.0, 0.0).astype(BF16)
            cores = [(terms[h, core] * keep).reshape(NX * NZ * 16, HEAD) for core in range(NS)]
            both = jnp.concatenate(cores, axis=1)
            part = dot(emb_t[...], both)
            for core in range(NS):
                at = (other * NS + core) * CHUNK + h * HEAD
                mod_out[:, at : at + HEAD] = part[:, core * HEAD : (core + 1) * HEAD]

    head(0)
    along_y(0)
    give_back(0, dq_s, dq_out, 0)
    pass_on(2)
    head(1)
    along_y(1)
    give_back(0, dq_s, dq_out, 1)
    finish(0)
    along_z(0)
    head(2)
    along_y(2)
    along_x(0)
    along_z(1)
    give_back(0, dq_s, dq_out, 2)
    finish(1)
    along_x(1)
    to_core(0)
    along_z(2)
    finish(2)
    along_x(2)
    to_core(1)
    contract(0)
    to_core(2)
    contract(1)
    contract(2)

    outs = (dq_out, dk_out, dv_out)
    arrived = pl.ds(0, (GROUP - 1) * CHUNK)
    for a in range(3):
        wait(outs[a].at[:, arrived], o_recv.at[a])
        wait(outs[a].at[:, arrived], o_send.at[a])
    for a in range(4):
        for h in range(MINE):
            wait(q_in.at[:, pl.ds(0, (GROUP - 1) * HEAD)], in_send.at[a, h])
    for h in range(MINE):
        wait(kb.at[h, pl.ds(0, SPAN)], z_send.at[0, h])
        wait(vb.at[h, pl.ds(0, SPAN)], z_send.at[1, h])
        for n in range(2):
            wait(halo_s.at[h, n], h_send.at[n, h])
    wait(meta.at[pl.ds(0, NY - 1)], m_send.at[0])
    wait(times.at[0, pl.ds(0, NZ - 1)], m_send.at[1])
    wait(times.at[pl.ds(0, NX - 1)], m_send.at[2])
    for h in range(MINE):
        wait(rows_y.at[h, pl.ds(0, NY - 1)], t_send.at[0, h])
        wait(terms.at[h, 0, 0, pl.ds(0, NZ - 1)], t_send.at[1, h])
        wait(terms.at[h, 0, pl.ds(0, NX - 1)], t_send.at[2, h])
        wait(terms.at[h, 0], t_send.at[3, h])


def store_kernel(dq, dk, dv, mod, dq_out, dk_out, dv_out, mod_out, sems):
    pairs = ((mod, mod_out), (dq, dq_out), (dk, dk_out), (dv, dv_out))
    copies = [pltpu.make_async_copy(src, dst, sems.at[n]) for n, (src, dst) in enumerate(pairs)]
    for copy in copies:
        copy.start()
    for copy in copies:
        copy.wait()


def in_vmem(array):
    return pltpu.with_memory_space_constraint(array, pltpu.VMEM)


def in_hbm(array):
    return pltpu.with_memory_space_constraint(array, pltpu.HBM)


def local(
    queries, key_states, value_states, out_grad, head_slopes, timesteps, stretch_frames,
    valid_counts, mod_weight,
):
    flat = (PART, WIDTH)
    anywhere = pl.BlockSpec(memory_space=pl.ANY)
    smem = pl.BlockSpec(memory_space=pltpu.SMEM)
    hbm = pl.BlockSpec(memory_space=pltpu.HBM)
    dma = pltpu.SemaphoreType.DMA
    grad = jax.ShapeDtypeStruct(flat, BF16)
    dq, dk, dv, mod = pl.pallas_call(
        main_kernel,
        name="attention_backward",
        out_shape=(pltpu.VMEM(flat, BF16),) * 3 + (pltpu.VMEM((FREQ, WIDTH), F32),),
        in_specs=[smem] * 4 + [hbm] * 5,
        out_specs=(pl.BlockSpec(memory_space=pltpu.VMEM),) * 4,
        scratch_shapes=[
            pltpu.VMEM((MINE, NY, TOK, HEAD), BF16),
            pltpu.VMEM((MINE, SLOTS, TOK, HEAD), BF16),
            pltpu.VMEM((MINE, SLOTS, TOK, HEAD), BF16),
            pltpu.VMEM((MINE, NY, TOK, HEAD), BF16),
            pltpu.VMEM((HEAD, SLOTS * TOK), BF16),
            pltpu.VMEM((HEAD, SLOTS * TOK), BF16),
            pltpu.VMEM((FREQ, CHUNK), F32),
            pltpu.VMEM((NY, 8, HEAD), jnp.int32),
            pltpu.VMEM((NX, NZ, NY, 8, HEAD), jnp.int32),
            pltpu.VMEM((NX * NZ * NY, HEAD), F32),
            pltpu.VMEM((MINE, 8, HEAD), F32),
            pltpu.VMEM((NX * NZ * 16, FREQ), F32),
            pltpu.VMEM((FREQ, NX * NZ * 16), BF16),
            pltpu.VMEM((SLOTS, TOK, HEAD), F32),
            pltpu.VMEM((SPAN + 1, TOK, TOK), F32),
            pltpu.VMEM((SPAN + 1, TOK, TOK), BF16),
            pltpu.VMEM((SPAN + 1, TOK, TOK), BF16),
            pltpu.VMEM((MINE, SLOTS, TOK, HEAD), F32),
            pltpu.VMEM((MINE, SLOTS, TOK, HEAD), F32),
            pltpu.VMEM((MINE, NY, TOK, HEAD), BF16),
            pltpu.VMEM((MINE, NY, TOK, HEAD), BF16),
            pltpu.VMEM((MINE, NY, TOK, HEAD), BF16),
            pltpu.VMEM((MINE, 2, SPAN, TOK, HEAD), BF16),
            pltpu.VMEM((MINE, 2, SPAN, TOK, HEAD), BF16),
            pltpu.VMEM((MINE, 16, HEAD), F32),
            pltpu.VMEM((MINE, NY, 16, HEAD), BF16),
            pltpu.VMEM((MINE, NS, NX, NZ, 16, HEAD), BF16),
            dma((4, MINE)), dma((4, MINE)),
            dma((2, MINE)), dma((2, MINE)),
            dma((2, MINE)), dma((2, MINE)),
            dma((3,)), dma((3,)),
            dma((3,)), dma((3,)),
            dma((4, MINE)), dma((4, MINE)),
            dma,
        ],
        compiler_params=pltpu.CompilerParams(
            collective_id=0, has_side_effects=True, vmem_limit_bytes=48 * 2**20
        ),
    )(
        in_hbm(head_slopes), timesteps, stretch_frames,
        valid_counts, in_hbm(mod_weight), in_hbm(queries.reshape(flat)),
        in_hbm(key_states.reshape(flat)), in_hbm(value_states.reshape(flat)),
        in_hbm(out_grad.reshape(flat)),
    )
    dq, dk, dv, mod = pl.pallas_call(
        store_kernel,
        name="store",
        out_shape=(pltpu.HBM(flat, BF16),) * 3 + (pltpu.HBM((FREQ, WIDTH), F32),),
        in_specs=[pl.BlockSpec(memory_space=pltpu.VMEM)] * 4,
        out_specs=(anywhere,) * 4,
        scratch_shapes=[dma((4,))],
        compiler_params=pltpu.CompilerParams(vmem_limit_bytes=4 * 2**20),
    )(in_vmem(dq), in_vmem(dk), in_vmem(dv), in_vmem(mod))
    whole = (1, 1, PART, WIDTH)
    return dq.reshape(whole), dk.reshape(whole), dv.reshape(whole), mod


def solution(mesh):
    tokens = P("dp", "frame", "spatial", None)
    each = P("dp", "frame")
    return jax.shard_map(
        local,
        mesh=mesh,
        in_specs=(tokens, tokens, tokens, tokens, P(), each, each, each, P()),
        out_specs=(tokens, tokens, tokens, P()),
        check_vma=False,
    )
```
